32 devices in a mesh: elem: 8 (over y, x, core), band: 4 (over z).
Axes of the slice: x: 2, y: 2, z: 4, core: 2. Of those that a mesh axis runs over, the one named last changes fastest.
Arguments:
- state: bfloat16 [16384, 256], P(('elem', 'band')), may hold values from -6 to 6
- dest_map: int32 [16384, 1], P(('elem', 'band')), may hold values from 0 to 7; in each aligned block of 512 rows (0 to 511, 512 to 1023, ...) at most 128 rows name the same one
- day_mask: int32 [16384, 1], P(('elem', 'band')), may hold values 0 or 1
- cloud: bfloat16 [32768, 512], P(('elem', 'band')), may hold values from -6 to 6
- conv_in: bfloat16 [768, 256], replicated, may hold values from -0.21875 to 0.21875
- conv_mid: bfloat16 [256, 256], replicated, may hold values from -0.375 to 0.375
- conv_out: bfloat16 [256, 768], replicated, may hold values from -0.375 to 0.375
- rad_in: bfloat16 [768, 256], replicated, may hold values from -0.21875 to 0.21875
- rad_mid: bfloat16 [256, 256], replicated, may hold values from -0.375 to 0.375
- rad_out: bfloat16 [256, 128], replicated, may hold values from -0.375 to 0.375
Outputs:
- tendency: bfloat16 [16384, 256], P(('elem', 'band'))
- new_cloud: bfloat16 [32768, 512], P(('elem', 'band'))
The draws below stay inside these ranges and needn't reach their ends.
Inputs may be any that keep to these rules, and one draw needn't show every extreme that they name: `dest_map`: among the columns of one device (aligned blocks of 512 rows) no value is named by more than 128 rows, a bound that some block reaches.
All inputs are finite; a program needn't handle non-finite values. No bound on the sum of `day_mask` on one device may be relied on, other than what follows from the above.
Results may differ from the reference program's by a relative error of at most 0.0058.
Values may be sent and summed in bfloat16 or wider, within the bound.
No kernel may reach another device: no remote copies, remote signals or barrier semaphores. Data moves between devices by JAX's collectives and lax.ppermute only.
A program may use at most 64 MiB of HBM per device.

```python
import math
import jax
import jax.numpy as jnp
import numpy as np
from jax import lax

LEV = 128
HID = 256
COL_DEV = 512
CAP = 128
SLOTS = 1024
COLS = 16384
SPAN_ROWS = 32768
N_ELEM = 8
N_BAND = 4


def place_ends(values, rng, low, top_value):
    longest = values.shape.index(max(values.shape))
    spots = []
    for shift in (0, 1):
        where = [jax.random.randint(jax.random.fold_in(rng, axis), (), 0, length) for axis, length in enumerate(values.shape)]
        where[longest] = (where[longest] + shift) % values.shape[longest]
        spots.append(tuple(where))
    return values.at[spots[0]].set(low).at[spots[1]].set(top_value)


def block_levels(key, shape, shards, low, high):
    factor_of = 1.0
    for dim, blocks in shards:
        steps = jax.random.uniform(jax.random.fold_in(jax.random.fold_in(key, 6), dim), (blocks,), jnp.float32, low / len(shards), high / len(shards))
        factor_of = factor_of * jnp.repeat(jnp.exp(steps), shape[dim] // blocks).reshape((-1,) + (1,) * (len(shape) - 1 - dim))
    return factor_of


def shared_out(stream_key, own, number, rows, amount, top, most, skew):
    sequence = jax.random.permutation(stream_key, amount)
    packed, usual = shares(amount, rows * top, most, skew, True), shares(amount, rows * top, most, skew, False)
    places = jnp.arange(amount)

    def named(tallies, offset_by):
        used = int((tallies > 0).sum())
        fixed = max(1, used // 4)
        moved = fixed + (places - fixed + offset_by * (used - fixed)) % max(1, amount - fixed)
        return jnp.zeros((amount,), jnp.int32).at[sequence[jnp.where(places < fixed, places, moved)]].set(jnp.asarray(tallies, jnp.int32))

    tallies = jnp.where(number % 4 == 0, named(packed, number // 4), named(usual, number - number // 4 - 1))
    mixed = jax.random.permutation(jax.random.fold_in(own, 3), amount)
    giver, taker = mixed[0:amount // 2 * 2:2], mixed[1:amount // 2 * 2:2]
    margin = jnp.minimum(tallies[giver] - 1, most - tallies[taker]) // 2
    margin = jnp.where((giver == sequence[0]) | (taker == sequence[0]) | (tallies[taker] == 0), 0, jnp.maximum(margin, 0))
    moved = jax.random.randint(jax.random.fold_in(own, 4), (amount // 2,), 0, 1 << 20) % (margin + 1)
    tallies = tallies.at[giver].add(-moved).at[taker].add(moved)
    labels = jnp.searchsorted(jnp.cumsum(tallies), jnp.arange(rows * top), side="right").astype(jnp.int32)
    grid = labels.reshape(top, rows).T
    grid = grid[jax.random.permutation(jax.random.fold_in(own, 1), rows)]
    offset_by = jax.random.randint(jax.random.fold_in(own, 2), (rows, 1), 0, top)
    return jnp.take_along_axis(grid, (jnp.arange(top)[None, :] + offset_by) % top, axis=1)


def shares(amount, total, limit, slope, full):
    portions = [(1 << 20) // math.isqrt(rank ** slope) + 1 for rank in range(1, amount + 1)]
    largest = limit if full else min(limit, max(-(-total // amount), total * portions[0] // sum(portions)))
    least = 1 if total - largest >= amount - 1 else 0
    given, surplus = [largest] + [least] * (amount - 1), total - largest - least * (amount - 1)
    while surplus > 0:
        free = [i for i in range(1, amount) if given[i] < largest] or [i for i in range(1, amount) if given[i] < limit]
        pool, budget = sum([portions[i] for i in free]), surplus
        for i in free:
            more = min(limit - given[i], max(1, budget * portions[i] // pool), surplus)
            given[i] = given[i] + more
            surplus = surplus - more
    return np.array(given)


def noise(rng, dims, deviation, most, split=(), held_as=jnp.bfloat16):
    drawn = deviation * jax.random.normal(rng, dims, jnp.float32)
    if split:
        drawn = drawn * block_levels(rng, dims, split, -0.22, 0.18)
    return jnp.clip(drawn, -most, most).astype(held_as)


def setup_inputs(seed: int = 0) -> dict:
    arg_keys = jax.random.split(jax.random.key(seed), 11)
    state = noise(arg_keys[0], (COLS, 2 * LEV), 1.0, 6.0, ((0, 32),))
    dest_map_keys = jax.random.split(jax.random.fold_in(arg_keys[1], 1), COLS // COL_DEV)
    dest_map_turns = jax.random.permutation(jax.random.fold_in(arg_keys[1], 3), COLS // COL_DEV)
    dest_map = jax.vmap(lambda own, number: shared_out(jax.random.fold_in(arg_keys[1], 2), own, number, COL_DEV, N_ELEM, 1, CAP, 2))(dest_map_keys, dest_map_turns).reshape((COLS, 1))
    day_mask = place_ends((jax.random.randint(arg_keys[2], (COLS, 1), 0, 2) < 1).astype(jnp.int32), jax.random.fold_in(arg_keys[2], 1), 0, 1)
    cloud = noise(arg_keys[3], (SPAN_ROWS, 4 * LEV), 1.0, 6.0, ((0, 32),))
    conv_in = noise(arg_keys[4], (6 * LEV, HID), (6 * LEV) ** -0.5, 0.21875)
    conv_mid = noise(arg_keys[5], (HID, HID), HID ** -0.5, 0.375)
    conv_out = noise(arg_keys[6], (HID, 6 * LEV), HID ** -0.5, 0.375)
    rad_in = noise(arg_keys[7], (6 * LEV, HID), (6 * LEV) ** -0.5, 0.21875)
    rad_mid = noise(arg_keys[8], (HID, HID), HID ** -0.5, 0.375)
    rad_out = noise(arg_keys[9], (HID, LEV), HID ** -0.5, 0.375)
    return {"state": state, "dest_map": dest_map, "day_mask": day_mask, "cloud": cloud, "conv_in": conv_in, "conv_mid": conv_mid, "conv_out": conv_out, "rad_in": rad_in, "rad_mid": rad_mid, "rad_out": rad_out}


def column_physics(joined, daylight, cloud, conv_in, conv_mid, conv_out, rad_in, rad_mid, rad_out):
    conv_one = jax.nn.silu(jnp.dot(joined, conv_in, preferred_element_type=jnp.float32)).astype(jnp.bfloat16)
    conv_two = jax.nn.silu(jnp.dot(conv_one, conv_mid, preferred_element_type=jnp.float32)).astype(jnp.bfloat16)
    conv_result = jnp.dot(conv_two, conv_out, preferred_element_type=jnp.float32)
    rad_one = jax.nn.silu(jnp.dot(joined, rad_in, preferred_element_type=jnp.float32)).astype(jnp.bfloat16)
    rad_two = jax.nn.silu(jnp.dot(rad_one, rad_mid, preferred_element_type=jnp.float32)).astype(jnp.bfloat16)
    rad_result = jnp.dot(rad_two, rad_out, preferred_element_type=jnp.float32)
    heating = daylight[:, None] * rad_result
    padded = jnp.concatenate([heating, jnp.zeros_like(heating)], axis=1)
    tendency_rows = (conv_result[:, :2 * LEV] + padded).astype(jnp.bfloat16)
    updated = (cloud.astype(jnp.float32) + conv_result[:, 2 * LEV:]).astype(jnp.bfloat16)
    return tendency_rows, updated


def reference(state, dest_map, day_mask, cloud, conv_in, conv_mid, conv_out, rad_in, rad_mid, rad_out):
    target = dest_map[:, 0].reshape(N_ELEM, N_BAND, COL_DEV)
    onehot = (target[..., None] == jnp.arange(N_ELEM, dtype=jnp.int32)).astype(jnp.int32)
    order_in = jnp.sum((jnp.cumsum(onehot, axis=2) - onehot) * onehot, axis=-1)
    elem_index = jnp.arange(N_ELEM, dtype=jnp.int32)[:, None, None]
    band_index = jnp.arange(N_BAND, dtype=jnp.int32)[None, :, None]
    served_band = jnp.where(elem_index >= N_ELEM // 2, (band_index + N_BAND // 2) % N_BAND, band_index)
    span_row = ((target * N_BAND + served_band) * SLOTS + elem_index * CAP + order_in).reshape(-1).astype(jnp.int32)
    span_state = jnp.zeros((SPAN_ROWS, 2 * LEV), jnp.bfloat16).at[span_row].set(state)
    span_day = jnp.zeros((SPAN_ROWS,), jnp.float32).at[span_row].set(day_mask[:, 0].astype(jnp.float32))
    blocks = N_ELEM * N_BAND

    def one_block(pieces):
        block_state, block_day, block_cloud = pieces
        joined = jnp.concatenate([block_state, block_cloud], axis=1)
        return column_physics(joined, block_day, block_cloud, conv_in, conv_mid, conv_out, rad_in, rad_mid, rad_out)

    span_tendency, new_cloud = lax.map(one_block, (span_state.reshape(blocks, SLOTS, 2 * LEV), span_day.reshape(blocks, SLOTS), cloud.reshape(blocks, SLOTS, 4 * LEV)))
    span_tendency = span_tendency.reshape(SPAN_ROWS, 2 * LEV)
    new_cloud = new_cloud.reshape(SPAN_ROWS, 4 * LEV)
    tendency = span_tendency[span_row]
    return tendency, new_cloud
```

```python
import functools

import jax
import jax.numpy as jnp
from jax import lax
from jax.experimental import pallas as pl
from jax.experimental.pallas import tpu as pltpu
from jax.sharding import PartitionSpec as P

VMEM_BYTES = 20 * 1024 * 1024
FLAG_ROWS = 16


def moved(block, target):
    groups, bands = lax.axis_size("elem"), lax.axis_size("band")
    route = []
    for e in range(groups):
        for b in range(bands):
            to_elem, to_band = target(e, b)
            route.append((e * bands + b, to_elem * bands + to_band))
    return lax.ppermute(block, ("elem", "band"), route)


def orders(dest, groups):
    count = dest.shape[1]
    lanes = 128
    hot = (lax.broadcasted_iota(jnp.int32, (groups, count), 0) == dest).astype(jnp.float32)
    before = (
        lax.broadcasted_iota(jnp.int32, (lanes, lanes), 0)
        < lax.broadcasted_iota(jnp.int32, (lanes, lanes), 1)
    ).astype(jnp.bfloat16)
    parts, seen = [], jnp.zeros((groups, 1), jnp.float32)
    for start in range(0, count, lanes):
        piece = hot[:, start : start + lanes]
        inside = jnp.dot(piece.astype(jnp.bfloat16), before, preferred_element_type=jnp.float32)
        parts.append(jnp.sum(piece * (inside + seen), axis=0, keepdims=True))
        seen = seen + jnp.sum(piece, axis=1, keepdims=True)
    return jnp.concatenate(parts, axis=1).astype(jnp.int32)


def place_kernel(groups, cap, ids_ref, maps_ref, far_maps_ref, state_ref, far_state_ref, order_ref, *out_refs):
    core, unit = ids_ref[0], ids_ref[1]
    units = groups // 2
    columns, features = state_ref.shape
    flags = []
    for far, (maps, rows) in enumerate(((maps_ref, state_ref), (far_maps_ref, far_state_ref))):
        source_core = core if far == 0 else 1 - core
        dest, day = maps[0:1, :], maps[1:2, :]
        order = orders(dest, groups)
        if far == 0:
            order_ref[...] = jnp.concatenate([dest, order] + [jnp.zeros_like(dest)] * 6, axis=0)
        step = lax.bitwise_xor(lax.shift_right_logical(dest, 1), jnp.full_like(dest, unit))
        row = jnp.where(lax.bitwise_and(dest, 1) == core, step * cap + order, -1)
        hot = (lax.broadcasted_iota(jnp.int32, (units * cap, columns), 0) == row).astype(jnp.bfloat16)
        placed = jnp.dot(hot, rows[...], preferred_element_type=jnp.float32).astype(jnp.bfloat16)
        sun = jnp.broadcast_to(day.astype(jnp.float32), (FLAG_ROWS, columns)).astype(jnp.bfloat16)
        flags.append(
            lax.dot_general(sun, hot, (((1,), (1,)), ((), ())), preferred_element_type=jnp.float32)
        )
        for du in range(units):
            out_refs[du][pl.ds(pl.multiple_of(source_core * cap, cap), cap), :] = placed[du * cap : (du + 1) * cap, :]
    first = jnp.where(core == 0, flags[0], flags[1]).astype(jnp.bfloat16)
    second = jnp.where(core == 0, flags[1], flags[0]).astype(jnp.bfloat16)
    middle = features // 2
    for du in range(units):
        if cap < middle:
            out_refs[du][2 * cap :, :] = jnp.zeros((FLAG_ROWS, features), jnp.bfloat16)
        out_refs[du][2 * cap :, 0:cap] = first[:, du * cap : (du + 1) * cap]
        out_refs[du][2 * cap :, middle : middle + cap] = second[:, du * cap : (du + 1) * cap]


def silu(v):
    return (0.5 * v) * (1.0 + jnp.tanh(0.5 * v))


def dot(a, b):
    return jnp.dot(a, b, preferred_element_type=jnp.float32)


def as_column(row, cap):
    same = lax.broadcasted_iota(jnp.int32, (cap, cap), 0) == lax.broadcasted_iota(jnp.int32, (cap, cap), 1)
    return jnp.sum(jnp.where(same, jnp.broadcast_to(row, (cap, cap)), 0.0), axis=1, keepdims=True)


def physics_kernel(cap, has_base, ids_ref, near_ref, cross_ref, lent_ref, cloud_ref, conv_in, conv_mid, conv_out, rad_in, rad_mid, rad_out, *rest):
    straight_ref, crossed_ref, new_ref = rest[1:] if has_base else rest
    step = pl.program_id(0)
    upper = ids_ref[2]
    features = near_ref.shape[1]
    levels = rad_out.shape[1]

    def serve(packet, out_ref):
        state = packet[0 : 2 * cap, :]
        cloud = cloud_ref[...]
        conv = silu(dot(state, conv_in[:features, :]) + dot(cloud, conv_in[features:, :])).astype(jnp.bfloat16)
        rad = silu(dot(state, rad_in[:features, :]) + dot(cloud, rad_in[features:, :])).astype(jnp.bfloat16)
        conv = silu(dot(conv, conv_mid[...])).astype(jnp.bfloat16)
        rad = silu(dot(rad, rad_mid[...])).astype(jnp.bfloat16)
        conv = dot(conv, conv_out[...])
        rad = dot(rad, rad_out[...])
        flags = packet[2 * cap : 2 * cap + FLAG_ROWS, :].astype(jnp.float32)[0:1, :]
        middle = features // 2
        day = jnp.concatenate(
            [as_column(flags[:, 0:cap], cap), as_column(flags[:, middle : middle + cap], cap)], axis=0
        )
        out_ref[:, :levels] = (conv[:, :levels] + day * rad).astype(jnp.bfloat16)
        out_ref[:, levels:] = conv[:, levels : 2 * levels].astype(jnp.bfloat16)
        new_ref[...] = (cloud.astype(jnp.float32) + conv[:, 2 * levels :]).astype(jnp.bfloat16)

    @pl.when(jnp.logical_and(step == 0, upper == 0))
    def _():
        serve(near_ref, straight_ref)

    @pl.when(jnp.logical_and(step == 0, upper == 1))
    def _():
        serve(cross_ref, crossed_ref)

    @pl.when(jnp.logical_and(step == 1, upper == 0))
    def _():
        serve(lent_ref, crossed_ref)

    @pl.when(jnp.logical_and(step == 1, upper == 1))
    def _():
        serve(lent_ref, straight_ref)


def collect_kernel(groups, cap, ids_ref, order_ref, *refs):
    units = groups // 2
    core, unit = ids_ref[0], ids_ref[1]
    own, far, out_ref = refs[:units], refs[units : 2 * units], refs[2 * units]
    table = jnp.transpose(order_ref[...].astype(jnp.float32)).astype(jnp.int32)
    dest, order = table[:, 0:1], table[:, 1:2]
    step = lax.bitwise_xor(lax.shift_right_logical(dest, 1), jnp.full_like(dest, unit))
    side = jnp.where(lax.bitwise_and(dest, 1) == core, 0, 1)
    row = (step * 2 + side) * cap + order
    columns = dest.shape[0]
    total = jnp.zeros((columns, out_ref.shape[1]), jnp.float32)
    offset = pl.multiple_of(core * cap, cap)
    for du in range(units):
        hot = (lax.broadcasted_iota(jnp.int32, (columns, 2 * cap), 1) + 2 * du * cap == row).astype(jnp.bfloat16)
        block = jnp.concatenate([own[du][pl.ds(offset, cap), :], far[du][pl.ds(offset, cap), :]], axis=0)
        total = total + dot(hot, block)
    out_ref[...] = total.astype(jnp.bfloat16)


def per_device(state, dest_map, day_mask, cloud, conv_in, conv_mid, conv_out, rad_in, rad_mid, rad_out):
    groups, bands = lax.axis_size("elem"), lax.axis_size("band")
    units, half, away = groups // 2, groups // 4, bands // 2
    cap = cloud.shape[0] // groups
    columns, features = state.shape
    elem = lax.axis_index("elem")
    core, unit = elem % 2, elem // 2
    upper = (unit >= half).astype(jnp.int32)
    ids = jnp.stack([core, unit, upper]).astype(jnp.int32)
    smem = pl.BlockSpec(memory_space=pltpu.SMEM)
    vmem = pl.BlockSpec(memory_space=pltpu.VMEM)
    params = pltpu.CompilerParams(vmem_limit_bytes=VMEM_BYTES)

    def swapped(block):
        return moved(block, lambda e, b: (e ^ 1, b))

    maps = jnp.concatenate([dest_map.reshape(1, columns), day_mask.reshape(1, columns)], axis=0)
    far_maps = swapped(maps)
    far_state = swapped(state)

    packet = jax.ShapeDtypeStruct((2 * cap + FLAG_ROWS, features), jnp.bfloat16)
    order, *packets = pl.pallas_call(
        functools.partial(place_kernel, groups, cap),
        out_shape=[jax.ShapeDtypeStruct((8, columns), jnp.int32)] + [packet] * units,
        in_specs=[smem] + [vmem] * 4,
        out_specs=[vmem] * (units + 1),
        compiler_params=params,
        name="place_columns",
    )(ids, maps, far_maps, state, far_state)

    came = [packets[0]] + [None] * (units - 1)
    for low in range(half):
        for du in (half + low, low):
            if du:
                came[du] = moved(packets[du], lambda e, b: (e ^ (2 * du), b))

    lent = []
    for low in range(half):
        leaving = jnp.where(upper == 0, came[half + low], came[low])
        lent.append(moved(leaving, lambda e, b: (e, (b + away) % bands)))

    answers = [None] * units
    new_cloud = None
    tile = jax.ShapeDtypeStruct((2 * cap, features), jnp.bfloat16)
    weights = (conv_in, conv_mid, conv_out, rad_in, rad_mid, rad_out)
    whole = lambda a: pl.BlockSpec(a.shape, lambda i, ids: (0, 0))
    for low in range(half):
        lower_unit = (unit % half) ^ low
        call_ids = jnp.stack([lower_unit, half + lower_unit, upper]).astype(jnp.int32)
        cloud_spec = pl.BlockSpec((2 * cap, cloud.shape[1]), lambda i, ids: (ids[i], 0))
        base = () if new_cloud is None else (new_cloud,)
        args = (came[low], came[half + low], lent[low], cloud) + weights + base
        answers[low], answers[half + low], new_cloud = pl.pallas_call(
            functools.partial(physics_kernel, cap, bool(base)),
            grid_spec=pltpu.PrefetchScalarGridSpec(
                num_scalar_prefetch=1,
                grid=(2,),
                in_specs=[whole(came[low])] * 3 + [cloud_spec] + [whole(w) for w in weights]
                + [pl.BlockSpec(memory_space=pl.ANY)] * len(base),
                out_specs=[pl.BlockSpec(tile.shape, lambda i, ids: (0, 0))] * 2 + [cloud_spec],
            ),
            out_shape=[tile, tile, jax.ShapeDtypeStruct(cloud.shape, jnp.bfloat16)],
            input_output_aliases={len(args): 2} if base else {},
            compiler_params=params,
            name="column_physics",
        )(call_ids, *args)

    def home(du):
        def target(e, b):
            to_elem = e ^ (2 * du)
            return to_elem, (b + away) % bands if to_elem >= groups // 2 else b

        return target

    back, far_back = [None] * units, [None] * units
    for low in range(half):
        for du in (low, half + low):
            back[du] = moved(answers[du], home(du))
            far_back[du] = swapped(back[du])

    tendency = pl.pallas_call(
        functools.partial(collect_kernel, groups, cap),
        out_shape=jax.ShapeDtypeStruct(state.shape, jnp.bfloat16),
        in_specs=[smem] + [vmem] * (2 * units + 1),
        out_specs=vmem,
        compiler_params=params,
        name="collect_columns",
    )(ids, order, *back, *far_back)
    return (tendency, new_cloud)


def solution(mesh):
    rows = P(("elem", "band"), None)
    return jax.shard_map(
        per_device,
        mesh=mesh,
        in_specs=(rows,) * 4 + (P(),) * 6,
        out_specs=(rows, rows),
        check_vma=False,
    )
```

```python
import functools

import jax
import jax.numpy as jnp
from jax import lax
from jax.experimental import pallas as pl
from jax.experimental.pallas import tpu as pltpu
from jax.sharding import PartitionSpec as P

VMEM_BYTES = 24 * 1024 * 1024
FLAG_ROWS = 16


def moved(block, target):
    groups, bands = lax.axis_size("elem"), lax.axis_size("band")
    route = []
    for e in range(groups):
        for b in range(bands):
            to = target(e, b)
            if to is not None:
                route.append((e * bands + b, to[0] * bands + to[1]))
    return lax.ppermute(block, ("elem", "band"), route)


def work(microseconds):
    return pl.CostEstimate(flops=int(microseconds * 1.15e9), bytes_accessed=0, transcendentals=0)


def dot(a, b):
    return jnp.dot(a, b, preferred_element_type=jnp.float32)


def as_row(table):
    return jnp.concatenate([table[r : r + 1, :] for r in range(table.shape[0])], axis=1)


def orders(dest, groups):
    count = dest.shape[1]
    lanes = 128
    hot = (lax.broadcasted_iota(jnp.int32, (groups, count), 0) == dest).astype(jnp.float32)
    before = (
        lax.broadcasted_iota(jnp.int32, (lanes, lanes), 0)
        < lax.broadcasted_iota(jnp.int32, (lanes, lanes), 1)
    ).astype(jnp.bfloat16)
    parts, seen = [], jnp.zeros((groups, 1), jnp.float32)
    for start in range(0, count, lanes):
        piece = hot[:, start : start + lanes]
        inside = dot(piece.astype(jnp.bfloat16), before)
        parts.append(jnp.sum(piece * (inside + seen), axis=0, keepdims=True))
        seen = seen + jnp.sum(piece, axis=1, keepdims=True)
    return jnp.concatenate(parts, axis=1).astype(jnp.int32)


def place_kernel(groups, cap, ids_ref, far_dest_ref, far_day_ref, far_state_ref, *refs):
    units = groups // 2
    dest_ref, day_ref, state_ref, order_ref, *out_refs = refs
    core, unit = ids_ref[0], ids_ref[1]
    columns, features = state_ref.shape
    flags = []
    for far, (dest_table, day_table, rows) in enumerate(
        ((dest_ref, day_ref, state_ref), (far_dest_ref, far_day_ref, far_state_ref))
    ):
        source_core = core if far == 0 else 1 - core
        dest, day = as_row(dest_table[...]), as_row(day_table[...])
        order = orders(dest, groups)
        if far == 0:
            order_ref[...] = jnp.concatenate([dest, order] + [jnp.zeros_like(dest)] * 6, axis=0)
        step = lax.bitwise_xor(lax.shift_right_logical(dest, 1), jnp.full_like(dest, unit))
        row = jnp.where(lax.bitwise_and(dest, 1) == core, step * cap + order, -1)
        hot = (lax.broadcasted_iota(jnp.int32, (units * cap, columns), 0) == row).astype(jnp.bfloat16)
        sun = jnp.broadcast_to(day.astype(jnp.float32), (FLAG_ROWS, columns)).astype(jnp.bfloat16)
        flags.append(
            lax.dot_general(sun, hot, (((1,), (1,)), ((), ())), preferred_element_type=jnp.float32)
        )
        placed = dot(hot, rows[...]).astype(jnp.bfloat16)
        for du in range(units):
            out_refs[du][pl.ds(pl.multiple_of(source_core * cap, cap), cap), :] = placed[du * cap : (du + 1) * cap, :]
    first = jnp.where(core == 0, flags[0], flags[1]).astype(jnp.bfloat16)
    second = jnp.where(core == 0, flags[1], flags[0]).astype(jnp.bfloat16)
    middle = features // 2
    for du in range(units):
        if cap < middle:
            out_refs[du][2 * cap :, :] = jnp.zeros((FLAG_ROWS, features), jnp.bfloat16)
        out_refs[du][2 * cap :, 0:cap] = first[:, du * cap : (du + 1) * cap]
        out_refs[du][2 * cap :, middle : middle + cap] = second[:, du * cap : (du + 1) * cap]


def silu(v):
    return (0.5 * v) * (1.0 + jnp.tanh(0.5 * v))


def as_column(row, cap):
    same = lax.broadcasted_iota(jnp.int32, (cap, cap), 0) == lax.broadcasted_iota(jnp.int32, (cap, cap), 1)
    return jnp.sum(jnp.where(same, jnp.broadcast_to(row, (cap, cap)), 0.0), axis=1, keepdims=True)


def serve(cap, packet, cloud, weights):
    conv_in, conv_mid, conv_out, rad_in, rad_mid, rad_out = weights
    features, levels = packet.shape[1], rad_out.shape[1]
    state = packet[0 : 2 * cap, :]
    conv = silu(dot(state, conv_in[:features, :]) + dot(cloud, conv_in[features:, :])).astype(jnp.bfloat16)
    rad = silu(dot(state, rad_in[:features, :]) + dot(cloud, rad_in[features:, :])).astype(jnp.bfloat16)
    conv = silu(dot(conv, conv_mid[...])).astype(jnp.bfloat16)
    rad = silu(dot(rad, rad_mid[...])).astype(jnp.bfloat16)
    conv = dot(conv, conv_out[...])
    rad = dot(rad, rad_out[...])
    updated = (cloud.astype(jnp.float32) + conv[:, 2 * levels :]).astype(jnp.bfloat16)
    flags = packet[2 * cap : 2 * cap + FLAG_ROWS, :].astype(jnp.float32)[0:1, :]
    middle = features // 2
    day = jnp.concatenate(
        [as_column(flags[:, 0:cap], cap), as_column(flags[:, middle : middle + cap], cap)], axis=0
    )
    heated = conv[:, :levels] + day * rad
    return jnp.concatenate([heated, conv[:, levels : 2 * levels]], axis=1).astype(jnp.bfloat16), updated


def rows_of(unit, cap):
    return pl.ds(pl.multiple_of(unit * 2 * cap, 2 * cap), 2 * cap)


def lower_kernel(groups, cap, base, pick, ids_ref, order_ref, *refs):
    near, cross, cloud_ref, weights, refs = refs[0:2], refs[2:4], refs[4], refs[5:11], refs[11 + base :]
    answers, new_ref, refs = refs[0:2], refs[2], refs[3:]
    core, unit, upper, lower_unit = ids_ref[0], ids_ref[1], ids_ref[2], ids_ref[3]
    packet_ref, updated_ref, sems = refs[-3:]
    copies = []
    for i in range(2):

        @pl.when(upper == 0)
        def _():
            packet_ref[...] = near[i][...]

        @pl.when(upper == 1)
        def _():
            packet_ref[...] = cross[i][...]

        served = rows_of(lax.bitwise_xor(lower_unit, i), cap)
        answers[i][...], updated_ref[i] = serve(cap, packet_ref, cloud_ref[served, :], weights)
        copies.append(pltpu.make_async_copy(updated_ref.at[i], new_ref.at[served, :], sems.at[i]))
        copies[-1].start()
    if pick:
        hot_ref = refs[0]
        table = jnp.transpose(order_ref[...].astype(jnp.float32)).astype(jnp.int32)
        dest, order = table[:, 0:1], table[:, 1:2]
        step = lax.bitwise_xor(lax.shift_right_logical(dest, 1), jnp.full_like(dest, unit))
        side = jnp.where(lax.bitwise_and(dest, 1) == core, 0, 1)
        row = (step * 2 + side) * cap + order
        hot_ref[...] = (lax.broadcasted_iota(jnp.int32, hot_ref.shape, 1) == row).astype(jnp.bfloat16)
    for copy in copies:
        copy.wait()


def upper_kernel(cap, ids_ref, lent_ref, lower_answer_ref, cloud_ref, *refs):
    weights, (straight_ref, crossed_ref, new_ref) = refs[:6], refs[6:]
    upper, upper_unit = ids_ref[2], ids_ref[4]
    answer, new_ref[...] = serve(cap, lent_ref, cloud_ref[rows_of(upper_unit, cap), :], weights)

    @pl.when(upper == 0)
    def _():
        crossed_ref[...] = answer
        straight_ref[...] = lower_answer_ref[...]

    @pl.when(upper == 1)
    def _():
        straight_ref[...] = answer
        crossed_ref[...] = lower_answer_ref[...]


def collect_kernel(groups, cap, ids_ref, hot_ref, *refs):
    units = groups // 2
    half = units // 2
    own, far, news, refs = refs[:units], refs[units : 2 * units], refs[2 * units : 2 * units + half], refs[2 * units + half + 1 :]
    out_ref, new_ref, sems = refs
    core, upper_unit = ids_ref[0], ids_ref[4]
    copies = []
    for low, piece in enumerate(news):
        served = lax.bitwise_xor(upper_unit, low)
        copies.append(pltpu.make_async_copy(piece, new_ref.at[rows_of(served, cap), :], sems.at[low]))
        copies[-1].start()
    offset = pl.multiple_of(core * cap, cap)
    total = None
    for du in range(units):
        block = jnp.concatenate([own[du][pl.ds(offset, cap), :], far[du][pl.ds(offset, cap), :]], axis=0)
        part = dot(hot_ref[:, 2 * du * cap : 2 * (du + 1) * cap], block)
        total = part if total is None else total + part
    out_ref[...] = total.astype(jnp.bfloat16)
    for copy in copies:
        copy.wait()


def per_device(state, dest_map, day_mask, cloud, conv_in, conv_mid, conv_out, rad_in, rad_mid, rad_out):
    groups, bands = lax.axis_size("elem"), lax.axis_size("band")
    units, half, away = groups // 2, groups // 4, bands // 2
    cap = cloud.shape[0] // groups
    columns, features = state.shape
    elem = lax.axis_index("elem")
    core, unit = elem % 2, elem // 2
    upper = unit // half
    smem = pl.BlockSpec(memory_space=pltpu.SMEM)
    vmem = pl.BlockSpec(memory_space=pltpu.VMEM)
    hbm = pl.BlockSpec(memory_space=pltpu.HBM)
    params = pltpu.CompilerParams(vmem_limit_bytes=VMEM_BYTES)
    weights = (conv_in, conv_mid, conv_out, rad_in, rad_mid, rad_out)

    def ids_for(low):
        lower_unit = (unit % half) ^ low
        return jnp.stack([core, unit, upper, lower_unit, half + lower_unit]).astype(jnp.int32)

    def like(a):
        return jax.ShapeDtypeStruct(a.shape, a.dtype)

    def swapped(block):
        return moved(block, lambda e, b: (e ^ 1, b))

    ids = ids_for(0)
    dest_table, day_table = dest_map.reshape(columns // 128, 128), day_mask.reshape(columns // 128, 128)
    far_state = swapped(state)
    far_dest, far_day = swapped(dest_table), swapped(day_table)

    packet = jax.ShapeDtypeStruct((2 * cap + FLAG_ROWS, features), jnp.bfloat16)
    order, *packets = pl.pallas_call(
        functools.partial(place_kernel, groups, cap),
        out_shape=[jax.ShapeDtypeStruct((8, columns), jnp.int32)] + [packet] * units,
        in_specs=[smem] + [vmem] * 6,
        out_specs=[vmem] * (units + 1),
        compiler_params=params,
        cost_estimate=work(4),
        name="place_columns",
    )(ids, far_dest, far_day, far_state, dest_table, day_table, state)

    came = [packets[0]] + [None] * (units - 1)
    for low in range(half):
        for du in (half + low, low):
            if du:
                came[du] = moved(packets[du], lambda e, b: (e ^ (2 * du), b))
    lent = []
    for low in range(half):
        leaving = jnp.where(upper == 0, came[half + low], came[low])
        lent.append(moved(leaving, lambda e, b: (e, (b + away) % bands)))

    tile = jax.ShapeDtypeStruct((2 * cap, features), jnp.bfloat16)
    new_tile = jax.ShapeDtypeStruct((2 * cap, cloud.shape[1]), jnp.bfloat16)
    hot_shape = jax.ShapeDtypeStruct((columns, groups * cap), jnp.bfloat16)
    packet_buffer = pltpu.VMEM(packet.shape, jnp.bfloat16)
    answers, lower_answers, news, new_cloud = [None] * units, [], [], None
    for low in range(0, half, 2):
        pick, base = low == 0, () if low == 0 else (new_cloud,)
        outs = pl.pallas_call(
            functools.partial(lower_kernel, groups, cap, len(base), pick),
            out_shape=[tile, tile, like(cloud)] + [hot_shape] * pick,
            in_specs=[smem] + [vmem] * 12 + [hbm] * len(base),
            out_specs=[vmem, vmem, hbm] + [vmem] * pick,
            scratch_shapes=[packet_buffer, pltpu.VMEM((2,) + new_tile.shape, jnp.bfloat16), pltpu.SemaphoreType.DMA((2,))],
            input_output_aliases={13: 2} if base else {},
            compiler_params=params,
            cost_estimate=work(4),
            name="lower_physics",
        )(ids_for(low), order, came[low], came[low + 1], came[half + low], came[half + low + 1], cloud, *weights, *base)
        lower_answers += outs[0:2]
        new_cloud = outs[2]
        if pick:
            hot = outs[3]
    for low in range(half):
        answers[low], answers[half + low], new = pl.pallas_call(
            functools.partial(upper_kernel, cap),
            out_shape=[tile, tile, new_tile],
            in_specs=[smem] + [vmem] * 9,
            out_specs=[vmem] * 3,
            compiler_params=params,
            cost_estimate=work(3),
            name="upper_physics",
        )(ids_for(low), lent[low], lower_answers[low], cloud, *weights)
        news.append(new)

    def home(du):
        def target(e, b):
            to_elem = e ^ (2 * du)
            return to_elem, (b + away) % bands if to_elem >= groups // 2 else b

        return target

    back, far_back = [None] * units, [None] * units
    for low in range(half):
        for du in (half + low, low):
            back[du] = moved(answers[du], home(du))
    for du in range(units):
        far_back[du] = swapped(back[du])

    tendency, new_cloud = pl.pallas_call(
        functools.partial(collect_kernel, groups, cap),
        out_shape=[like(state), like(cloud)],
        in_specs=[smem] + [vmem] * (2 * units + half + 1) + [hbm],
        out_specs=[vmem, hbm],
        scratch_shapes=[pltpu.SemaphoreType.DMA((half,))],
        input_output_aliases={2 + 2 * units + half: 1},
        compiler_params=params,
        cost_estimate=work(3),
        name="collect_columns",
    )(ids, hot, *back, *far_back, *news, new_cloud)
    return (tendency, new_cloud)


def solution(mesh):
    rows = P(("elem", "band"), None)
    return jax.shard_map(
        per_device,
        mesh=mesh,
        in_specs=(rows,) * 4 + (P(),) * 6,
        out_specs=(rows, rows),
        check_vma=False,
    )
```

```python
import functools

import jax
import jax.numpy as jnp
from jax import lax
from jax.experimental import pallas as pl
from jax.experimental.pallas import tpu as pltpu
from jax.sharding import PartitionSpec as P

VMEM_BYTES = 24 * 1024 * 1024
FLAG_ROWS = 16


def moved(block, target):
    groups, bands = lax.axis_size("elem"), lax.axis_size("band")
    route = []
    for e in range(groups):
        for b in range(bands):
            to = target(e, b)
            if to is not None:
                route.append((e * bands + b, to[0] * bands + to[1]))
    return lax.ppermute(block, ("elem", "band"), route)


def work(microseconds):
    return pl.CostEstimate(flops=int(microseconds * 1.15e9), bytes_accessed=0, transcendentals=0)


def dot(a, b):
    return jnp.dot(a, b, preferred_element_type=jnp.float32)


def as_row(table):
    return jnp.concatenate([table[r : r + 1, :] for r in range(table.shape[0])], axis=1)


def orders(dest, groups):
    count = dest.shape[1]
    lanes = 128
    hot = (lax.broadcasted_iota(jnp.int32, (groups, count), 0) == dest).astype(jnp.float32)
    before = (
        lax.broadcasted_iota(jnp.int32, (lanes, lanes), 0)
        < lax.broadcasted_iota(jnp.int32, (lanes, lanes), 1)
    ).astype(jnp.bfloat16)
    parts, seen = [], jnp.zeros((groups, 1), jnp.float32)
    for start in range(0, count, lanes):
        piece = hot[:, start : start + lanes]
        inside = dot(piece.astype(jnp.bfloat16), before)
        parts.append(jnp.sum(piece * (inside + seen), axis=0, keepdims=True))
        seen = seen + jnp.sum(piece, axis=1, keepdims=True)
    return jnp.concatenate(parts, axis=1).astype(jnp.int32)


def targets_kernel(groups, cap, ids_ref, dest_ref, day_ref, far_dest_ref, far_day_ref, out_ref):
    core, unit = ids_ref[0], ids_ref[1]
    rows = []
    for dest_table, day_table in ((dest_ref, day_ref), (far_dest_ref, far_day_ref)):
        dest = as_row(dest_table[...])
        order = orders(dest, groups)
        step = lax.bitwise_xor(lax.shift_right_logical(dest, 1), jnp.full_like(dest, unit))
        rows += [jnp.where(lax.bitwise_and(dest, 1) == core, step * cap + order, -1), as_row(day_table[...]), dest, order]
    out_ref[...] = jnp.concatenate(rows, axis=0)


def place_kernel(groups, cap, ids_ref, targets_ref, state_ref, far_state_ref, *out_refs):
    core = ids_ref[0]
    units = groups // 2
    columns, features = state_ref.shape
    flags = []
    for far, rows in enumerate((state_ref, far_state_ref)):
        source_core = core if far == 0 else 1 - core
        row, day = targets_ref[4 * far : 4 * far + 1, :], targets_ref[4 * far + 1 : 4 * far + 2, :]
        hot = (lax.broadcasted_iota(jnp.int32, (units * cap, columns), 0) == row).astype(jnp.bfloat16)
        sun = jnp.broadcast_to(day.astype(jnp.float32), (FLAG_ROWS, columns)).astype(jnp.bfloat16)
        flags.append(
            lax.dot_general(sun, hot, (((1,), (1,)), ((), ())), preferred_element_type=jnp.float32)
        )
        placed = dot(hot, rows[...]).astype(jnp.bfloat16)
        for du in range(units):
            out_refs[du][pl.ds(pl.multiple_of(source_core * cap, cap), cap), :] = placed[du * cap : (du + 1) * cap, :]
    first = jnp.where(core == 0, flags[0], flags[1]).astype(jnp.bfloat16)
    second = jnp.where(core == 0, flags[1], flags[0]).astype(jnp.bfloat16)
    middle = features // 2
    for du in range(units):
        if cap < middle:
            out_refs[du][2 * cap :, :] = jnp.zeros((FLAG_ROWS, features), jnp.bfloat16)
        out_refs[du][2 * cap :, 0:cap] = first[:, du * cap : (du + 1) * cap]
        out_refs[du][2 * cap :, middle : middle + cap] = second[:, du * cap : (du + 1) * cap]


def silu(v):
    return (0.5 * v) * (1.0 + jnp.tanh(0.5 * v))


def as_column(row, cap):
    same = lax.broadcasted_iota(jnp.int32, (cap, cap), 0) == lax.broadcasted_iota(jnp.int32, (cap, cap), 1)
    return jnp.sum(jnp.where(same, jnp.broadcast_to(row, (cap, cap)), 0.0), axis=1, keepdims=True)


def serve(cap, packet, cloud, weights):
    conv_in, conv_mid, conv_out, rad_in, rad_mid, rad_out = weights
    features, levels = packet.shape[1], rad_out.shape[1]
    state = packet[0 : 2 * cap, :]
    conv = silu(dot(state, conv_in[:features, :]) + dot(cloud, conv_in[features:, :])).astype(jnp.bfloat16)
    rad = silu(dot(state, rad_in[:features, :]) + dot(cloud, rad_in[features:, :])).astype(jnp.bfloat16)
    conv = silu(dot(conv, conv_mid[...])).astype(jnp.bfloat16)
    rad = silu(dot(rad, rad_mid[...])).astype(jnp.bfloat16)
    conv = dot(conv, conv_out[...])
    rad = dot(rad, rad_out[...])
    updated = (cloud.astype(jnp.float32) + conv[:, 2 * levels :]).astype(jnp.bfloat16)
    flags = packet[2 * cap : 2 * cap + FLAG_ROWS, :].astype(jnp.float32)[0:1, :]
    middle = features // 2
    day = jnp.concatenate(
        [as_column(flags[:, 0:cap], cap), as_column(flags[:, middle : middle + cap], cap)], axis=0
    )
    heated = conv[:, :levels] + day * rad
    return jnp.concatenate([heated, conv[:, levels : 2 * levels]], axis=1).astype(jnp.bfloat16), updated


def rows_of(unit, cap):
    return pl.ds(pl.multiple_of(unit * 2 * cap, 2 * cap), 2 * cap)


def lower_kernel(groups, cap, base, pick, ids_ref, targets_ref, *refs):
    near, cross, cloud_ref, weights, refs = refs[0:2], refs[2:4], refs[4], refs[5:11], refs[11 + base :]
    answers, new_ref, refs = refs[0:2], refs[2], refs[3:]
    core, unit, upper, lower_unit = ids_ref[0], ids_ref[1], ids_ref[2], ids_ref[3]
    packet_ref, updated_ref, sems = refs[-3:]
    copies = []
    for i in range(2):

        @pl.when(upper == 0)
        def _():
            packet_ref[...] = near[i][...]

        @pl.when(upper == 1)
        def _():
            packet_ref[...] = cross[i][...]

        served = rows_of(lax.bitwise_xor(lower_unit, i), cap)
        answers[i][...], updated_ref[i] = serve(cap, packet_ref, cloud_ref[served, :], weights)
        copies.append(pltpu.make_async_copy(updated_ref.at[i], new_ref.at[served, :], sems.at[i]))
        copies[-1].start()
    if pick:
        hot_ref = refs[0]
        table = jnp.transpose(targets_ref[...].astype(jnp.float32)).astype(jnp.int32)
        dest, order = table[:, 2:3], table[:, 3:4]
        step = lax.bitwise_xor(lax.shift_right_logical(dest, 1), jnp.full_like(dest, unit))
        side = jnp.where(lax.bitwise_and(dest, 1) == core, 0, 1)
        row = (step * 2 + side) * cap + order
        hot_ref[...] = (lax.broadcasted_iota(jnp.int32, hot_ref.shape, 1) == row).astype(jnp.bfloat16)
    for copy in copies:
        copy.wait()


def upper_kernel(cap, ids_ref, lent_ref, lower_answer_ref, cloud_ref, *refs):
    weights, (straight_ref, crossed_ref, new_ref) = refs[:6], refs[6:]
    upper, upper_unit = ids_ref[2], ids_ref[4]
    answer, new_ref[...] = serve(cap, lent_ref, cloud_ref[rows_of(upper_unit, cap), :], weights)

    @pl.when(upper == 0)
    def _():
        crossed_ref[...] = answer
        straight_ref[...] = lower_answer_ref[...]

    @pl.when(upper == 1)
    def _():
        straight_ref[...] = answer
        crossed_ref[...] = lower_answer_ref[...]


def store_kernel(cap, ids_ref, *refs):
    news, (new_ref, sems) = refs[:-3], refs[-2:]
    copies = []
    for low, piece in enumerate(news):
        served = lax.bitwise_xor(ids_ref[4], low)
        copies.append(pltpu.make_async_copy(piece, new_ref.at[rows_of(served, cap), :], sems.at[low]))
        copies[-1].start()
    for copy in copies:
        copy.wait()


def collect_kernel(groups, cap, ids_ref, hot_ref, *refs):
    units = groups // 2
    own, far, out_ref = refs[:units], refs[units : 2 * units], refs[2 * units]
    offset = pl.multiple_of(ids_ref[0] * cap, cap)
    total = None
    for du in range(units):
        block = jnp.concatenate([own[du][pl.ds(offset, cap), :], far[du][pl.ds(offset, cap), :]], axis=0)
        part = dot(hot_ref[:, 2 * du * cap : 2 * (du + 1) * cap], block)
        total = part if total is None else total + part
    out_ref[...] = total.astype(jnp.bfloat16)


def per_device(state, dest_map, day_mask, cloud, conv_in, conv_mid, conv_out, rad_in, rad_mid, rad_out):
    groups, bands = lax.axis_size("elem"), lax.axis_size("band")
    units, half, away = groups // 2, groups // 4, bands // 2
    cap = cloud.shape[0] // groups
    columns, features = state.shape
    elem = lax.axis_index("elem")
    core, unit = elem % 2, elem // 2
    upper = unit // half
    smem = pl.BlockSpec(memory_space=pltpu.SMEM)
    vmem = pl.BlockSpec(memory_space=pltpu.VMEM)
    hbm = pl.BlockSpec(memory_space=pltpu.HBM)
    params = pltpu.CompilerParams(vmem_limit_bytes=VMEM_BYTES)
    weights = (conv_in, conv_mid, conv_out, rad_in, rad_mid, rad_out)

    def ids_for(low):
        lower_unit = (unit % half) ^ low
        return jnp.stack([core, unit, upper, lower_unit, half + lower_unit]).astype(jnp.int32)

    def like(a):
        return jax.ShapeDtypeStruct(a.shape, a.dtype)

    def swapped(block):
        return moved(block, lambda e, b: (e ^ 1, b))

    ids = ids_for(0)
    dest_table, day_table = dest_map.reshape(columns // 128, 128), day_mask.reshape(columns // 128, 128)
    far_state = swapped(state)
    far_dest, far_day = swapped(dest_table), swapped(day_table)

    packet = jax.ShapeDtypeStruct((2 * cap + FLAG_ROWS, features), jnp.bfloat16)
    targets = pl.pallas_call(
        functools.partial(targets_kernel, groups, cap),
        out_shape=jax.ShapeDtypeStruct((8, columns), jnp.int32),
        in_specs=[smem] + [vmem] * 4,
        out_specs=vmem,
        compiler_params=params,
        cost_estimate=work(4),
        name="column_targets",
    )(ids, dest_table, day_table, far_dest, far_day)
    packets = pl.pallas_call(
        functools.partial(place_kernel, groups, cap),
        out_shape=[packet] * units,
        in_specs=[smem] + [vmem] * 3,
        out_specs=[vmem] * units,
        compiler_params=params,
        cost_estimate=work(4),
        name="place_columns",
    )(ids, targets, state, far_state)

    came = [packets[0]] + [None] * (units - 1)
    for low in range(half):
        for du in (half + low, low):
            if du:
                came[du] = moved(packets[du], lambda e, b: (e ^ (2 * du), b))
    lent = []
    for low in range(half):
        leaving = jnp.where(upper == 0, came[half + low], came[low])
        lent.append(moved(leaving, lambda e, b: (e, (b + away) % bands)))

    tile = jax.ShapeDtypeStruct((2 * cap, features), jnp.bfloat16)
    new_tile = jax.ShapeDtypeStruct((2 * cap, cloud.shape[1]), jnp.bfloat16)
    hot_shape = jax.ShapeDtypeStruct((columns, groups * cap), jnp.bfloat16)
    packet_buffer = pltpu.VMEM(packet.shape, jnp.bfloat16)
    answers, lower_answers, news, new_cloud = [None] * units, [], [], None
    for low in range(0, half, 2):
        pick, base = low == 0, () if low == 0 else (new_cloud,)
        outs = pl.pallas_call(
            functools.partial(lower_kernel, groups, cap, len(base), pick),
            out_shape=[tile, tile, like(cloud)] + [hot_shape] * pick,
            in_specs=[smem] + [vmem] * 12 + [hbm] * len(base),
            out_specs=[vmem, vmem, hbm] + [vmem] * pick,
            scratch_shapes=[packet_buffer, pltpu.VMEM((2,) + new_tile.shape, jnp.bfloat16), pltpu.SemaphoreType.DMA((2,))],
            input_output_aliases={13: 2} if base else {},
            compiler_params=params,
            cost_estimate=work(4),
            name="lower_physics",
        )(ids_for(low), targets, came[low], came[low + 1], came[half + low], came[half + low + 1], cloud, *weights, *base)
        lower_answers += outs[0:2]
        new_cloud = outs[2]
        if pick:
            hot = outs[3]
    for low in range(half):
        answers[low], answers[half + low], new = pl.pallas_call(
            functools.partial(upper_kernel, cap),
            out_shape=[tile, tile, new_tile],
            in_specs=[smem] + [vmem] * 9,
            out_specs=[vmem] * 3,
            compiler_params=params,
            cost_estimate=work(3),
            name="upper_physics",
        )(ids_for(low), lent[low], lower_answers[low], cloud, *weights)
        news.append(new)

    def home(du):
        def target(e, b):
            to_elem = e ^ (2 * du)
            return to_elem, (b + away) % bands if to_elem >= groups // 2 else b

        return target

    back = [None] * units
    sequence = [*range(half, units), *range(half)]
    for du in sequence:
        back[du] = moved(answers[du], home(du))
    new_cloud = pl.pallas_call(
        functools.partial(store_kernel, cap),
        out_shape=like(cloud),
        in_specs=[smem] + [vmem] * half + [hbm],
        out_specs=hbm,
        scratch_shapes=[pltpu.SemaphoreType.DMA((half,))],
        input_output_aliases={1 + half: 0},
        compiler_params=params,
        cost_estimate=work(1),
        name="store_cloud",
    )(ids, *news, new_cloud)
    back[half], new_cloud = lax.optimization_barrier((back[half], new_cloud))
    far_back = [None] * units
    for du in sequence:
        far_back[du] = swapped(back[du])
    tendency = pl.pallas_call(
        functools.partial(collect_kernel, groups, cap),
        out_shape=like(state),
        in_specs=[smem] + [vmem] * (2 * units + 1),
        out_specs=vmem,
        compiler_params=params,
        cost_estimate=work(3),
        name="collect_columns",
    )(ids, hot, *back, *far_back)
    return (tendency, new_cloud)


def solution(mesh):
    rows = P(("elem", "band"), None)
    return jax.shard_map(
        per_device,
        mesh=mesh,
        in_specs=(rows,) * 4 + (P(),) * 6,
        out_specs=(rows, rows),
        check_vma=False,
    )
```

```python
import functools

import jax
import jax.numpy as jnp
from jax import lax
from jax.experimental import pallas as pl
from jax.experimental.pallas import tpu as pltpu
from jax.sharding import PartitionSpec as P

VMEM_BYTES = 24 * 1024 * 1024
FLAG_ROWS = 16


def moved(block, target):
    groups, bands = lax.axis_size("elem"), lax.axis_size("band")
    route = []
    for e in range(groups):
        for b in range(bands):
            to = target(e, b)
            if to is not None:
                route.append((e * bands + b, to[0] * bands + to[1]))
    return lax.ppermute(block, ("elem", "band"), route)


def work(microseconds):
    return pl.CostEstimate(flops=int(microseconds * 1.15e9), bytes_accessed=0, transcendentals=0)


def dot(a, b):
    return jnp.dot(a, b, preferred_element_type=jnp.float32)


def as_row(table):
    return jnp.concatenate([table[r : r + 1, :] for r in range(table.shape[0])], axis=1)


def orders(dest, groups):
    count = dest.shape[1]
    lanes = 128
    hot = (lax.broadcasted_iota(jnp.int32, (groups, count), 0) == dest).astype(jnp.float32)
    before = (
        lax.broadcasted_iota(jnp.int32, (lanes, lanes), 0)
        < lax.broadcasted_iota(jnp.int32, (lanes, lanes), 1)
    ).astype(jnp.bfloat16)
    parts, seen = [], jnp.zeros((groups, 1), jnp.float32)
    for start in range(0, count, lanes):
        piece = hot[:, start : start + lanes]
        inside = dot(piece.astype(jnp.bfloat16), before)
        parts.append(jnp.sum(piece * (inside + seen), axis=0, keepdims=True))
        seen = seen + jnp.sum(piece, axis=1, keepdims=True)
    return jnp.concatenate(parts, axis=1).astype(jnp.int32)


def targets_kernel(groups, cap, ids_ref, dest_ref, day_ref, far_dest_ref, far_day_ref, out_ref):
    core, unit = ids_ref[0], ids_ref[1]
    rows = []
    for dest_table, day_table in ((dest_ref, day_ref), (far_dest_ref, far_day_ref)):
        dest = as_row(dest_table[...])
        order = orders(dest, groups)
        step = lax.bitwise_xor(lax.shift_right_logical(dest, 1), jnp.full_like(dest, unit))
        rows += [jnp.where(lax.bitwise_and(dest, 1) == core, step * cap + order, -1), as_row(day_table[...]), dest, order]
    out_ref[...] = jnp.concatenate(rows, axis=0)


def place_kernel(groups, cap, ids_ref, targets_ref, state_ref, far_state_ref, *out_refs):
    core = ids_ref[0]
    units = groups // 2
    columns, features = state_ref.shape
    flags = []
    for far, rows in enumerate((state_ref, far_state_ref)):
        source_core = core if far == 0 else 1 - core
        row, day = targets_ref[4 * far : 4 * far + 1, :], targets_ref[4 * far + 1 : 4 * far + 2, :]
        hot = (lax.broadcasted_iota(jnp.int32, (units * cap, columns), 0) == row).astype(jnp.bfloat16)
        sun = jnp.broadcast_to(day.astype(jnp.float32), (FLAG_ROWS, columns)).astype(jnp.bfloat16)
        flags.append(
            lax.dot_general(sun, hot, (((1,), (1,)), ((), ())), preferred_element_type=jnp.float32)
        )
        placed = dot(hot, rows[...]).astype(jnp.bfloat16)
        for du in range(units):
            out_refs[du][pl.ds(pl.multiple_of(source_core * cap, cap), cap), :] = placed[du * cap : (du + 1) * cap, :]
    first = jnp.where(core == 0, flags[0], flags[1]).astype(jnp.bfloat16)
    second = jnp.where(core == 0, flags[1], flags[0]).astype(jnp.bfloat16)
    middle = features // 2
    for du in range(units):
        if cap < middle:
            out_refs[du][2 * cap :, :] = jnp.zeros((FLAG_ROWS, features), jnp.bfloat16)
        out_refs[du][2 * cap :, 0:cap] = first[:, du * cap : (du + 1) * cap]
        out_refs[du][2 * cap :, middle : middle + cap] = second[:, du * cap : (du + 1) * cap]


def silu(v):
    return (0.5 * v) * (1.0 + jnp.tanh(0.5 * v))


def as_column(row, cap):
    same = lax.broadcasted_iota(jnp.int32, (cap, cap), 0) == lax.broadcasted_iota(jnp.int32, (cap, cap), 1)
    return jnp.sum(jnp.where(same, jnp.broadcast_to(row, (cap, cap)), 0.0), axis=1, keepdims=True)


def serve(cap, packet, cloud, weights):
    conv_in, conv_mid, conv_out, rad_in, rad_mid, rad_out = weights
    features, levels = packet.shape[1], rad_out.shape[1]
    state = packet[0 : 2 * cap, :]
    conv = silu(dot(state, conv_in[:features, :]) + dot(cloud, conv_in[features:, :])).astype(jnp.bfloat16)
    rad = silu(dot(state, rad_in[:features, :]) + dot(cloud, rad_in[features:, :])).astype(jnp.bfloat16)
    conv = silu(dot(conv, conv_mid[...])).astype(jnp.bfloat16)
    rad = silu(dot(rad, rad_mid[...])).astype(jnp.bfloat16)
    conv = dot(conv, conv_out[...])
    rad = dot(rad, rad_out[...])
    updated = (cloud.astype(jnp.float32) + conv[:, 2 * levels :]).astype(jnp.bfloat16)
    flags = packet[2 * cap : 2 * cap + FLAG_ROWS, :].astype(jnp.float32)[0:1, :]
    middle = features // 2
    day = jnp.concatenate(
        [as_column(flags[:, 0:cap], cap), as_column(flags[:, middle : middle + cap], cap)], axis=0
    )
    heated = conv[:, :levels] + day * rad
    return jnp.concatenate([heated, conv[:, levels : 2 * levels]], axis=1).astype(jnp.bfloat16), updated


def rows_of(unit, cap):
    return pl.ds(pl.multiple_of(unit * 2 * cap, 2 * cap), 2 * cap)


def lower_kernel(groups, cap, base, pick, ids_ref, targets_ref, *refs):
    near, cross, cloud_ref, weights, refs = refs[0:2], refs[2:4], refs[4], refs[5:11], refs[11 + base :]
    answers, new_ref, refs = refs[0:2], refs[2], refs[3:]
    core, unit, upper, lower_unit = ids_ref[0], ids_ref[1], ids_ref[2], ids_ref[3]
    packet_ref, updated_ref, sems = refs[-3:]
    copies = []
    for i in range(2):

        @pl.when(upper == 0)
        def _():
            packet_ref[...] = near[i][...]

        @pl.when(upper == 1)
        def _():
            packet_ref[...] = cross[i][...]

        served = rows_of(lax.bitwise_xor(lower_unit, i), cap)
        answers[i][...], updated_ref[i] = serve(cap, packet_ref, cloud_ref[served, :], weights)
        copies.append(pltpu.make_async_copy(updated_ref.at[i], new_ref.at[served, :], sems.at[i]))
        copies[-1].start()
    if pick:
        hot_ref = refs[0]
        table = jnp.transpose(targets_ref[...].astype(jnp.float32)).astype(jnp.int32)
        dest, order = table[:, 2:3], table[:, 3:4]
        step = lax.bitwise_xor(lax.shift_right_logical(dest, 1), jnp.full_like(dest, unit))
        side = jnp.where(lax.bitwise_and(dest, 1) == core, 0, 1)
        row = (step * 2 + side) * cap + order
        hot_ref[...] = (lax.broadcasted_iota(jnp.int32, hot_ref.shape, 1) == row).astype(jnp.bfloat16)
    for copy in copies:
        copy.wait()


def upper_kernel(cap, ids_ref, lent_ref, lower_answer_ref, cloud_ref, *refs):
    weights, (straight_ref, crossed_ref, new_ref) = refs[:6], refs[6:]
    upper, upper_unit = ids_ref[2], ids_ref[4]
    answer, new_ref[...] = serve(cap, lent_ref, cloud_ref[rows_of(upper_unit, cap), :], weights)

    @pl.when(upper == 0)
    def _():
        crossed_ref[...] = answer
        straight_ref[...] = lower_answer_ref[...]

    @pl.when(upper == 1)
    def _():
        straight_ref[...] = answer
        crossed_ref[...] = lower_answer_ref[...]


def store_kernel(cap, ids_ref, *refs):
    news, (new_ref, sems) = refs[:-3], refs[-2:]
    copies = []
    for low, piece in enumerate(news):
        served = lax.bitwise_xor(ids_ref[4], low)
        copies.append(pltpu.make_async_copy(piece, new_ref.at[rows_of(served, cap), :], sems.at[low]))
        copies[-1].start()
    for copy in copies:
        copy.wait()


def gathered(cap, hot_ref, pieces):
    total = None
    for place, blocks in pieces:
        block = blocks[0] if len(blocks) == 1 else jnp.concatenate(blocks, axis=0)
        part = dot(hot_ref[:, place * cap : (place + len(blocks)) * cap], block)
        total = part if total is None else total + part
    return total


def gather_kernel(cap, sequence, ids_ref, hot_ref, *refs):
    count = len(sequence)
    own, far, out_ref = refs[:count], refs[count:-1], refs[-1]
    rows = pl.ds(pl.multiple_of(ids_ref[0] * cap, cap), cap)
    pieces = []
    for i, du in enumerate(sequence):
        blocks = [own[i][rows, :]] + ([far[i][rows, :]] if i < count - 1 else [])
        pieces.append((2 * du, blocks))
    out_ref[...] = gathered(cap, hot_ref, pieces).astype(jnp.bfloat16)


def finish_kernel(cap, last, ids_ref, hot_ref, gathered_ref, far_ref, out_ref, buffer_ref, sems):
    block = far_ref[pl.ds(pl.multiple_of(ids_ref[0] * cap, cap), cap), :]
    parts = sems.shape[0]
    step = out_ref.shape[0] // parts
    copies = []
    for i in range(parts):
        span = pl.ds(i * step, step)
        part = dot(hot_ref[span, (2 * last + 1) * cap : (2 * last + 2) * cap], block)
        buffer_ref[span, :] = (gathered_ref[span, :].astype(jnp.float32) + part).astype(jnp.bfloat16)
        copies.append(pltpu.make_async_copy(buffer_ref.at[span, :], out_ref.at[span, :], sems.at[i]))
        copies[-1].start()
    for copy in copies:
        copy.wait()


def per_device(state, dest_map, day_mask, cloud, conv_in, conv_mid, conv_out, rad_in, rad_mid, rad_out):
    groups, bands = lax.axis_size("elem"), lax.axis_size("band")
    units, half, away = groups // 2, groups // 4, bands // 2
    cap = cloud.shape[0] // groups
    columns, features = state.shape
    elem = lax.axis_index("elem")
    core, unit = elem % 2, elem // 2
    upper = unit // half
    smem = pl.BlockSpec(memory_space=pltpu.SMEM)
    vmem = pl.BlockSpec(memory_space=pltpu.VMEM)
    hbm = pl.BlockSpec(memory_space=pltpu.HBM)
    params = pltpu.CompilerParams(vmem_limit_bytes=VMEM_BYTES)
    weights = (conv_in, conv_mid, conv_out, rad_in, rad_mid, rad_out)

    def ids_for(low):
        lower_unit = (unit % half) ^ low
        return jnp.stack([core, unit, upper, lower_unit, half + lower_unit]).astype(jnp.int32)

    def like(a):
        return jax.ShapeDtypeStruct(a.shape, a.dtype)

    def swapped(block):
        return moved(block, lambda e, b: (e ^ 1, b))

    ids = ids_for(0)
    dest_table, day_table = dest_map.reshape(columns // 128, 128), day_mask.reshape(columns // 128, 128)
    far_state = swapped(state)
    far_dest, far_day = swapped(dest_table), swapped(day_table)

    packet = jax.ShapeDtypeStruct((2 * cap + FLAG_ROWS, features), jnp.bfloat16)
    targets = pl.pallas_call(
        functools.partial(targets_kernel, groups, cap),
        out_shape=jax.ShapeDtypeStruct((8, columns), jnp.int32),
        in_specs=[smem] + [vmem] * 4,
        out_specs=vmem,
        compiler_params=params,
        cost_estimate=work(4),
        name="column_targets",
    )(ids, dest_table, day_table, far_dest, far_day)
    packets = pl.pallas_call(
        functools.partial(place_kernel, groups, cap),
        out_shape=[packet] * units,
        in_specs=[smem] + [vmem] * 3,
        out_specs=[vmem] * units,
        compiler_params=params,
        cost_estimate=work(4),
        name="place_columns",
    )(ids, targets, state, far_state)

    came = [packets[0]] + [None] * (units - 1)
    for low in range(half):
        for du in (half + low, low):
            if du:
                came[du] = moved(packets[du], lambda e, b: (e ^ (2 * du), b))
    lent = []
    for low in range(half):
        leaving = jnp.where(upper == 0, came[half + low], came[low])
        lent.append(moved(leaving, lambda e, b: (e, (b + away) % bands)))

    tile = jax.ShapeDtypeStruct((2 * cap, features), jnp.bfloat16)
    new_tile = jax.ShapeDtypeStruct((2 * cap, cloud.shape[1]), jnp.bfloat16)
    hot_shape = jax.ShapeDtypeStruct((columns, groups * cap), jnp.bfloat16)
    packet_buffer = pltpu.VMEM(packet.shape, jnp.bfloat16)
    answers, lower_answers, news, new_cloud = [None] * units, [], [], None
    for low in range(0, half, 2):
        pick, base = low == 0, () if low == 0 else (new_cloud,)
        outs = pl.pallas_call(
            functools.partial(lower_kernel, groups, cap, len(base), pick),
            out_shape=[tile, tile, like(cloud)] + [hot_shape] * pick,
            in_specs=[smem] + [vmem] * 12 + [hbm] * len(base),
            out_specs=[vmem, vmem, hbm] + [vmem] * pick,
            scratch_shapes=[packet_buffer, pltpu.VMEM((2,) + new_tile.shape, jnp.bfloat16), pltpu.SemaphoreType.DMA((2,))],
            input_output_aliases={13: 2} if base else {},
            compiler_params=params,
            cost_estimate=work(4),
            name="lower_physics",
        )(ids_for(low), targets, came[low], came[low + 1], came[half + low], came[half + low + 1], cloud, *weights, *base)
        lower_answers += outs[0:2]
        new_cloud = outs[2]
        if pick:
            hot = outs[3]
    for low in range(half):
        answers[low], answers[half + low], new = pl.pallas_call(
            functools.partial(upper_kernel, cap),
            out_shape=[tile, tile, new_tile],
            in_specs=[smem] + [vmem] * 9,
            out_specs=[vmem] * 3,
            compiler_params=params,
            cost_estimate=work(3),
            name="upper_physics",
        )(ids_for(low), lent[low], lower_answers[low], cloud, *weights)
        news.append(new)

    def home(du):
        def target(e, b):
            to_elem = e ^ (2 * du)
            return to_elem, (b + away) % bands if to_elem >= groups // 2 else b

        return target

    back = [None] * units
    sequence = [du for low in range(half) for du in (half + low, low)]
    back = [moved(answers[du], home(du)) for du in sequence]
    new_cloud = pl.pallas_call(
        functools.partial(store_kernel, cap),
        out_shape=like(cloud),
        in_specs=[smem] + [vmem] * half + [hbm],
        out_specs=hbm,
        scratch_shapes=[pltpu.SemaphoreType.DMA((half,))],
        input_output_aliases={1 + half: 0},
        compiler_params=params,
        cost_estimate=work(1),
        name="store_cloud",
    )(ids, *news, new_cloud)
    back[0], new_cloud = lax.optimization_barrier((back[0], new_cloud))
    far_back = [swapped(block) for block in back]
    most = pl.pallas_call(
        functools.partial(gather_kernel, cap, sequence),
        out_shape=like(state),
        in_specs=[smem] + [vmem] * (2 * units),
        out_specs=vmem,
        compiler_params=params,
        cost_estimate=work(2),
        name="gather_most",
    )(ids, hot, *back, *far_back[:-1])
    tendency = pl.pallas_call(
        functools.partial(finish_kernel, cap, sequence[-1]),
        out_shape=like(state),
        in_specs=[smem] + [vmem] * 3,
        out_specs=hbm,
        scratch_shapes=[pltpu.VMEM(state.shape, jnp.bfloat16), pltpu.SemaphoreType.DMA((2,))],
        compiler_params=params,
        cost_estimate=work(1),
        name="gather_last",
    )(ids, hot, most, far_back[-1])
    return (tendency, new_cloud)


def solution(mesh):
    rows = P(("elem", "band"), None)
    return jax.shard_map(
        per_device,
        mesh=mesh,
        in_specs=(rows,) * 4 + (P(),) * 6,
        out_specs=(rows, rows),
        check_vma=False,
    )
```

```python
import functools

import jax
import jax.numpy as jnp
from jax import lax
from jax.experimental import pallas as pl
from jax.experimental.pallas import tpu as pltpu
from jax.sharding import PartitionSpec as P

VMEM_BYTES = 24 * 1024 * 1024
FLAG_ROWS = 16


def moved(block, target):
    groups, bands = lax.axis_size("elem"), lax.axis_size("band")
    route = []
    for e in range(groups):
        for b in range(bands):
            to = target(e, b)
            if to is not None:
                route.append((e * bands + b, to[0] * bands + to[1]))
    return lax.ppermute(block, ("elem", "band"), route)


def work(microseconds):
    return pl.CostEstimate(flops=int(microseconds * 1.15e9), bytes_accessed=0, transcendentals=0)


def position():
    elem, half = lax.axis_index("elem"), lax.axis_size("elem") // 4
    unit = elem // 2
    return elem % 2, unit, unit // half, unit % half


def dot(a, b):
    return jnp.dot(a, b, preferred_element_type=jnp.float32)


def as_row(table):
    return jnp.concatenate([table[r : r + 1, :] for r in range(table.shape[0])], axis=1)


def orders(dest, groups):
    count = dest.shape[1]
    lanes = 128
    hot = (lax.broadcasted_iota(jnp.int32, (groups, count), 0) == dest).astype(jnp.float32)
    before = (
        lax.broadcasted_iota(jnp.int32, (lanes, lanes), 0)
        < lax.broadcasted_iota(jnp.int32, (lanes, lanes), 1)
    ).astype(jnp.bfloat16)
    parts, seen = [], jnp.zeros((groups, 1), jnp.float32)
    for start in range(0, count, lanes):
        piece = hot[:, start : start + lanes]
        inside = dot(piece.astype(jnp.bfloat16), before)
        parts.append(jnp.sum(piece * (inside + seen), axis=0, keepdims=True))
        seen = seen + jnp.sum(piece, axis=1, keepdims=True)
    return jnp.concatenate(parts, axis=1).astype(jnp.int32)


def targets_kernel(groups, cap, dest_ref, far_dest_ref, out_ref):
    core, unit, _, _ = position()
    rows = []
    for dest_table in (dest_ref, far_dest_ref):
        dest = as_row(dest_table[...])
        order = orders(dest, groups)
        step = lax.bitwise_xor(lax.shift_right_logical(dest, 1), jnp.full_like(dest, unit))
        rows += [jnp.where(lax.bitwise_and(dest, 1) == core, step * cap + order, -1), dest, order, dest]
    out_ref[...] = jnp.concatenate(rows, axis=0)


def place_kernel(cap, units, first_du, targets_ref, state_ref, far_state_ref, day_ref, far_day_ref, *refs):
    core, _, _, _ = position()
    out_refs = refs if len(refs) == 1 else refs[1:]
    count = len(out_refs) * cap
    columns, features = state_ref.shape
    flags = []
    for far, (rows, day_table) in enumerate(((state_ref, day_ref), (far_state_ref, far_day_ref))):
        source_core = core if far == 0 else 1 - core
        row, day = targets_ref[4 * far : 4 * far + 1, :], as_row(day_table[...])
        row = jnp.where(row < first_du * cap, jnp.where(row < 0, row, row + units * cap), row) - first_du * cap
        hot = (lax.broadcasted_iota(jnp.int32, (count, columns), 0) == row).astype(jnp.bfloat16)
        sun = jnp.broadcast_to(day.astype(jnp.float32), (FLAG_ROWS, columns)).astype(jnp.bfloat16)
        flags.append(
            lax.dot_general(sun, hot, (((1,), (1,)), ((), ())), preferred_element_type=jnp.float32)
        )
        placed = dot(hot, rows[...]).astype(jnp.bfloat16)
        for i, out_ref in enumerate(out_refs):
            out_ref[pl.ds(pl.multiple_of(source_core * cap, cap), cap), :] = placed[i * cap : (i + 1) * cap, :]
    first = jnp.where(core == 0, flags[0], flags[1]).astype(jnp.bfloat16)
    second = jnp.where(core == 0, flags[1], flags[0]).astype(jnp.bfloat16)
    middle = features // 2
    for i, out_ref in enumerate(out_refs):
        if cap < middle:
            out_ref[2 * cap :, :] = jnp.zeros((FLAG_ROWS, features), jnp.bfloat16)
        out_ref[2 * cap :, 0:cap] = first[:, i * cap : (i + 1) * cap]
        out_ref[2 * cap :, middle : middle + cap] = second[:, i * cap : (i + 1) * cap]


def silu(v):
    return (0.5 * v) * (1.0 + jnp.tanh(0.5 * v))


def as_column(row, cap):
    same = lax.broadcasted_iota(jnp.int32, (cap, cap), 0) == lax.broadcasted_iota(jnp.int32, (cap, cap), 1)
    return jnp.sum(jnp.where(same, jnp.broadcast_to(row, (cap, cap)), 0.0), axis=1, keepdims=True)


def cloud_part(cloud, weights, features):
    return [dot(cloud, weights[i][features:, :]) for i in (0, 3)]


def serve(cap, packet, cloud, first, weights):
    conv_in, conv_mid, conv_out, rad_in, rad_mid, rad_out = weights
    features, levels = packet.shape[1], rad_out.shape[1]
    state = packet[0 : 2 * cap, :]
    conv = silu(dot(state, conv_in[:features, :]) + first[0]).astype(jnp.bfloat16)
    rad = silu(dot(state, rad_in[:features, :]) + first[1]).astype(jnp.bfloat16)
    conv = silu(dot(conv, conv_mid[...])).astype(jnp.bfloat16)
    rad = silu(dot(rad, rad_mid[...])).astype(jnp.bfloat16)
    conv = dot(conv, conv_out[...])
    rad = dot(rad, rad_out[...])
    updated = (cloud.astype(jnp.float32) + conv[:, 2 * levels :]).astype(jnp.bfloat16)
    flags = packet[2 * cap : 2 * cap + FLAG_ROWS, :].astype(jnp.float32)[0:1, :]
    middle = features // 2
    day = jnp.concatenate(
        [as_column(flags[:, 0:cap], cap), as_column(flags[:, middle : middle + cap], cap)], axis=0
    )
    heated = conv[:, :levels] + day * rad
    return jnp.concatenate([heated, conv[:, levels : 2 * levels]], axis=1).astype(jnp.bfloat16), updated


def rows_of(unit, cap):
    return pl.ds(pl.multiple_of(unit * 2 * cap, 2 * cap), 2 * cap)


def lower_kernel(cap, base, pick, low, targets_ref, *refs):
    near, cross, cloud_ref, weights, refs = refs[0:2], refs[2:4], refs[4], refs[5:11], refs[11 + base :]
    answers, new_ref, firsts, refs = refs[0:2], refs[2], refs[3:5], refs[5:]
    core, unit, upper, inner = position()
    half = lax.axis_size("elem") // 4
    packet_ref, updated_ref, sems = refs[-3:]
    copies = []
    for i in range(2):

        @pl.when(upper == 0)
        def _():
            packet_ref[...] = near[i][...]

        @pl.when(upper == 1)
        def _():
            packet_ref[...] = cross[i][...]

        served = rows_of(lax.bitwise_xor(inner, low + i), cap)
        cloud = cloud_ref[served, :]
        answers[i][...], updated_ref[i] = serve(cap, packet_ref, cloud, cloud_part(cloud, weights, packet_ref.shape[1]), weights)
        copies.append(pltpu.make_async_copy(updated_ref.at[i], new_ref.at[served, :], sems.at[i]))
        copies[-1].start()
    for i, first_ref in enumerate(firsts):
        cloud = cloud_ref[rows_of(half + lax.bitwise_xor(inner, low + i), cap), :]
        for j, part in enumerate(cloud_part(cloud, weights, packet_ref.shape[1])):
            first_ref[j] = part
    if pick:
        hot_ref = refs[0]
        table = jnp.transpose(targets_ref[...].astype(jnp.float32)).astype(jnp.int32)
        dest, order = table[:, 1:2], table[:, 2:3]
        step = lax.bitwise_xor(lax.shift_right_logical(dest, 1), jnp.full_like(dest, unit))
        side = jnp.where(lax.bitwise_and(dest, 1) == core, 0, 1)
        row = (step * 2 + side) * cap + order
        hot_ref[...] = (lax.broadcasted_iota(jnp.int32, hot_ref.shape, 1) == row).astype(jnp.bfloat16)
    for copy in copies:
        copy.wait()


def upper_kernel(cap, low, lent_ref, lower_answer_ref, first_ref, cloud_ref, *refs):
    weights, (straight_ref, crossed_ref, new_ref) = refs[:6], refs[6:]
    _, _, upper, inner = position()
    upper_unit = lax.axis_size("elem") // 4 + lax.bitwise_xor(inner, low)
    answer, new_ref[...] = serve(cap, lent_ref, cloud_ref[rows_of(upper_unit, cap), :], first_ref, weights)

    @pl.when(upper == 0)
    def _():
        crossed_ref[...] = answer
        straight_ref[...] = lower_answer_ref[...]

    @pl.when(upper == 1)
    def _():
        straight_ref[...] = answer
        crossed_ref[...] = lower_answer_ref[...]


def store_kernel(cap, *refs):
    news, (new_ref, sems) = refs[:-3], refs[-2:]
    _, _, _, inner = position()
    copies = []
    for low, piece in enumerate(news):
        served = lax.axis_size("elem") // 4 + lax.bitwise_xor(inner, low)
        copies.append(pltpu.make_async_copy(piece, new_ref.at[rows_of(served, cap), :], sems.at[low]))
        copies[-1].start()
    for copy in copies:
        copy.wait()


def gathered(cap, hot_ref, pieces):
    total = None
    for place, blocks in pieces:
        block = blocks[0] if len(blocks) == 1 else jnp.concatenate(blocks, axis=0)
        part = dot(hot_ref[:, place * cap : (place + len(blocks)) * cap], block)
        total = part if total is None else total + part
    return total


def gather_kernel(cap, sequence, hot_ref, *refs):
    count = len(sequence)
    own, far, out_ref = refs[:count], refs[count:-1], refs[-1]
    rows = pl.ds(pl.multiple_of(position()[0] * cap, cap), cap)
    pieces = []
    for i, du in enumerate(sequence):
        blocks = [own[i][rows, :]] + ([far[i][rows, :]] if i < count - 1 else [])
        pieces.append((2 * du, blocks))
    out_ref[...] = gathered(cap, hot_ref, pieces).astype(jnp.bfloat16)


def finish_kernel(cap, last, hot_ref, gathered_ref, far_ref, out_ref, buffer_ref, sems):
    block = far_ref[pl.ds(pl.multiple_of(position()[0] * cap, cap), cap), :]
    parts = sems.shape[0]
    step = out_ref.shape[0] // parts
    copies = []
    for i in range(parts):
        span = pl.ds(i * step, step)
        part = dot(hot_ref[span, (2 * last + 1) * cap : (2 * last + 2) * cap], block)
        buffer_ref[span, :] = (gathered_ref[span, :].astype(jnp.float32) + part).astype(jnp.bfloat16)
        copies.append(pltpu.make_async_copy(buffer_ref.at[span, :], out_ref.at[span, :], sems.at[i]))
        copies[-1].start()
    for copy in copies:
        copy.wait()


def per_device(state, dest_map, day_mask, cloud, conv_in, conv_mid, conv_out, rad_in, rad_mid, rad_out):
    groups, bands = lax.axis_size("elem"), lax.axis_size("band")
    units, half, away = groups // 2, groups // 4, bands // 2
    cap = cloud.shape[0] // groups
    columns, features = state.shape
    elem = lax.axis_index("elem")
    upper = elem // (groups // 2)
    vmem = pl.BlockSpec(memory_space=pltpu.VMEM)
    hbm = pl.BlockSpec(memory_space=pltpu.HBM)
    params = pltpu.CompilerParams(vmem_limit_bytes=VMEM_BYTES)
    weights = (conv_in, conv_mid, conv_out, rad_in, rad_mid, rad_out)

    def like(a):
        return jax.ShapeDtypeStruct(a.shape, a.dtype)

    def swapped(block):
        return moved(block, lambda e, b: (e ^ 1, b))

    dest_table, day_table = dest_map.reshape(columns // 128, 128), day_mask.reshape(columns // 128, 128)
    far_state = swapped(state)
    far_dest, far_day = swapped(dest_table), swapped(day_table)

    packet = jax.ShapeDtypeStruct((2 * cap + FLAG_ROWS, features), jnp.bfloat16)
    targets = pl.pallas_call(
        functools.partial(targets_kernel, groups, cap),
        out_shape=jax.ShapeDtypeStruct((8, columns), jnp.int32),
        in_specs=[vmem] * 2,
        out_specs=vmem,
        compiler_params=params,
        cost_estimate=work(4),
        name="column_targets",
    )(dest_table, far_dest)
    packets = [None] * units
    for chosen in ([half], [*range(half + 1, units), *range(half)]):
        earlier = [packets[half]] if packets[half] is not None else []
        outs = pl.pallas_call(
            functools.partial(place_kernel, cap, units, chosen[0]),
            out_shape=[packet] * len(chosen),
            in_specs=[vmem] * (5 + len(earlier)),
            out_specs=[vmem] * len(chosen),
            compiler_params=params,
            cost_estimate=work(3),
            name="place_columns",
        )(targets, state, far_state, day_table, far_day, *earlier)
        for du, out in zip(chosen, outs):
            packets[du] = out

    came = [packets[0]] + [None] * (units - 1)
    for low in range(half):
        for du in (half + low, low):
            if du:
                came[du] = moved(packets[du], lambda e, b: (e ^ (2 * du), b))
    lent = []
    for low in range(half):
        leaving = jnp.where(upper == 0, came[half + low], came[low])
        lent.append(moved(leaving, lambda e, b: (e, (b + away) % bands)))

    tile = jax.ShapeDtypeStruct((2 * cap, features), jnp.bfloat16)
    new_tile = jax.ShapeDtypeStruct((2 * cap, cloud.shape[1]), jnp.bfloat16)
    first_shape = jax.ShapeDtypeStruct((2, 2 * cap, conv_in.shape[1]), jnp.float32)
    firsts = []
    hot_shape = jax.ShapeDtypeStruct((columns, groups * cap), jnp.bfloat16)
    packet_buffer = pltpu.VMEM(packet.shape, jnp.bfloat16)
    answers, lower_answers, news, new_cloud = [None] * units, [], [], None
    for low in range(0, half, 2):
        pick, base = low == 0, () if low == 0 else (new_cloud,)
        outs = pl.pallas_call(
            functools.partial(lower_kernel, cap, len(base), pick, low),
            out_shape=[tile, tile, like(cloud), first_shape, first_shape] + [hot_shape] * pick,
            in_specs=[vmem] * 12 + [hbm] * len(base),
            out_specs=[vmem, vmem, hbm, vmem, vmem] + [vmem] * pick,
            scratch_shapes=[packet_buffer, pltpu.VMEM((2,) + new_tile.shape, jnp.bfloat16), pltpu.SemaphoreType.DMA((2,))],
            input_output_aliases={12: 2} if base else {},
            compiler_params=params,
            cost_estimate=work(4),
            name="lower_physics",
        )(targets, came[low], came[low + 1], came[half + low], came[half + low + 1], cloud, *weights, *base)
        lower_answers += outs[0:2]
        new_cloud = outs[2]
        firsts += outs[3:5]
        if pick:
            hot = outs[5]
    for low in range(half):
        answers[low], answers[half + low], new = pl.pallas_call(
            functools.partial(upper_kernel, cap, low),
            out_shape=[tile, tile, new_tile],
            in_specs=[vmem] * 10,
            out_specs=[vmem] * 3,
            compiler_params=params,
            cost_estimate=work(3),
            name="upper_physics",
        )(lent[low], lower_answers[low], firsts[low], cloud, *weights)
        news.append(new)

    def home(du):
        def target(e, b):
            to_elem = e ^ (2 * du)
            return to_elem, (b + away) % bands if to_elem >= groups // 2 else b

        return target

    back = [None] * units
    sequence = [du for low in range(half) for du in (half + low, low)]
    back = [moved(answers[du], home(du)) for du in sequence]
    new_cloud = pl.pallas_call(
        functools.partial(store_kernel, cap),
        out_shape=like(cloud),
        in_specs=[vmem] * half + [hbm],
        out_specs=hbm,
        scratch_shapes=[pltpu.SemaphoreType.DMA((half,))],
        input_output_aliases={half: 0},
        compiler_params=params,
        cost_estimate=work(1),
        name="store_cloud",
    )(*news, new_cloud)
    back[0], new_cloud = lax.optimization_barrier((back[0], new_cloud))
    far_back = [swapped(block) for block in back]
    most = pl.pallas_call(
        functools.partial(gather_kernel, cap, sequence),
        out_shape=like(state),
        in_specs=[vmem] * (2 * units),
        out_specs=vmem,
        compiler_params=params,
        cost_estimate=work(2),
        name="gather_most",
    )(hot, *back, *far_back[:-1])
    tendency = pl.pallas_call(
        functools.partial(finish_kernel, cap, sequence[-1]),
        out_shape=like(state),
        in_specs=[vmem] * 3,
        out_specs=hbm,
        scratch_shapes=[pltpu.VMEM(state.shape, jnp.bfloat16), pltpu.SemaphoreType.DMA((2,))],
        compiler_params=params,
        cost_estimate=work(1),
        name="gather_last",
    )(hot, most, far_back[-1])
    return (tendency, new_cloud)


def solution(mesh):
    rows = P(("elem", "band"), None)
    return jax.shard_map(
        per_device,
        mesh=mesh,
        in_specs=(rows,) * 4 + (P(),) * 6,
        out_specs=(rows, rows),
        check_vma=False,
    )
```

```python
import functools

import jax
import jax.numpy as jnp
from jax import lax
from jax.experimental import pallas as pl
from jax.experimental.pallas import tpu as pltpu
from jax.sharding import PartitionSpec as P

VMEM_BYTES = 24 * 1024 * 1024
FLAG_ROWS = 16


def moved(block, target):
    groups, bands = lax.axis_size("elem"), lax.axis_size("band")
    route = []
    for e in range(groups):
        for b in range(bands):
            to = target(e, b)
            if to is not None:
                route.append((e * bands + b, to[0] * bands + to[1]))
    return lax.ppermute(block, ("elem", "band"), route)


def work(microseconds):
    return pl.CostEstimate(flops=int(microseconds * 1.15e9), bytes_accessed=0, transcendentals=0)


def position():
    elem, half = lax.axis_index("elem"), lax.axis_size("elem") // 4
    unit = elem // 2
    return elem % 2, unit, unit // half, unit % half


def dot(a, b):
    return jnp.dot(a, b, preferred_element_type=jnp.float32)


def as_row(table):
    return jnp.concatenate([table[r : r + 1, :] for r in range(table.shape[0])], axis=1)


def orders(dest, groups):
    count = dest.shape[1]
    lanes = 128
    hot = (lax.broadcasted_iota(jnp.int32, (groups, count), 0) == dest).astype(jnp.float32)
    before = (
        lax.broadcasted_iota(jnp.int32, (lanes, lanes), 0)
        < lax.broadcasted_iota(jnp.int32, (lanes, lanes), 1)
    ).astype(jnp.bfloat16)
    parts, seen = [], jnp.zeros((groups, 1), jnp.float32)
    for start in range(0, count, lanes):
        piece = hot[:, start : start + lanes]
        inside = dot(piece.astype(jnp.bfloat16), before)
        parts.append(jnp.sum(piece * (inside + seen), axis=0, keepdims=True))
        seen = seen + jnp.sum(piece, axis=1, keepdims=True)
    return jnp.concatenate(parts, axis=1).astype(jnp.int32)


def targets_kernel(groups, cap, dest_ref, far_dest_ref, out_ref):
    core, unit, _, _ = position()
    rows = []
    for dest_table in (dest_ref, far_dest_ref):
        dest = as_row(dest_table[...])
        order = orders(dest, groups)
        step = lax.bitwise_xor(lax.shift_right_logical(dest, 1), jnp.full_like(dest, unit))
        rows += [jnp.where(lax.bitwise_and(dest, 1) == core, step * cap + order, -1), dest, order, dest]
    out_ref[...] = jnp.concatenate(rows, axis=0)


def place_kernel(cap, units, first_du, far_state_ref, state_ref, targets_ref, far_day_ref, day_ref, *refs):
    core, _, _, _ = position()
    out_refs = refs if len(refs) == 1 else refs[1:]
    count = len(out_refs) * cap
    columns, features = state_ref.shape
    flags = []
    for far, (rows, day_table) in enumerate(((state_ref, day_ref), (far_state_ref, far_day_ref))):
        source_core = core if far == 0 else 1 - core
        row, day = targets_ref[4 * far : 4 * far + 1, :], as_row(day_table[...])
        row = jnp.where(row < first_du * cap, jnp.where(row < 0, row, row + units * cap), row) - first_du * cap
        hot = (lax.broadcasted_iota(jnp.int32, (count, columns), 0) == row).astype(jnp.bfloat16)
        sun = jnp.broadcast_to(day.astype(jnp.float32), (FLAG_ROWS, columns)).astype(jnp.bfloat16)
        flags.append(
            lax.dot_general(sun, hot, (((1,), (1,)), ((), ())), preferred_element_type=jnp.float32)
        )
        placed = dot(hot, rows[...]).astype(jnp.bfloat16)
        for i, out_ref in enumerate(out_refs):
            out_ref[pl.ds(pl.multiple_of(source_core * cap, cap), cap), :] = placed[i * cap : (i + 1) * cap, :]
    first = jnp.where(core == 0, flags[0], flags[1]).astype(jnp.bfloat16)
    second = jnp.where(core == 0, flags[1], flags[0]).astype(jnp.bfloat16)
    middle = features // 2
    for i, out_ref in enumerate(out_refs):
        if cap < middle:
            out_ref[2 * cap :, :] = jnp.zeros((FLAG_ROWS, features), jnp.bfloat16)
        out_ref[2 * cap :, 0:cap] = first[:, i * cap : (i + 1) * cap]
        out_ref[2 * cap :, middle : middle + cap] = second[:, i * cap : (i + 1) * cap]


def silu(v):
    return (0.5 * v) * (1.0 + jnp.tanh(0.5 * v))


def as_column(row, cap):
    same = lax.broadcasted_iota(jnp.int32, (cap, cap), 0) == lax.broadcasted_iota(jnp.int32, (cap, cap), 1)
    return jnp.sum(jnp.where(same, jnp.broadcast_to(row, (cap, cap)), 0.0), axis=1, keepdims=True)


def cloud_part(cloud, weights, features):
    return [dot(cloud, weights[i][features:, :]) for i in (0, 3)]


def serve(cap, packet, cloud, first, weights):
    conv_in, conv_mid, conv_out, rad_in, rad_mid, rad_out = weights
    features, levels = packet.shape[1], rad_out.shape[1]
    state = packet[0 : 2 * cap, :]
    conv = silu(dot(state, conv_in[:features, :]) + first[0]).astype(jnp.bfloat16)
    rad = silu(dot(state, rad_in[:features, :]) + first[1]).astype(jnp.bfloat16)
    conv = silu(dot(conv, conv_mid[...])).astype(jnp.bfloat16)
    rad = silu(dot(rad, rad_mid[...])).astype(jnp.bfloat16)
    conv = dot(conv, conv_out[...])
    rad = dot(rad, rad_out[...])
    updated = (cloud.astype(jnp.float32) + conv[:, 2 * levels :]).astype(jnp.bfloat16)
    flags = packet[2 * cap : 2 * cap + FLAG_ROWS, :].astype(jnp.float32)[0:1, :]
    middle = features // 2
    day = jnp.concatenate(
        [as_column(flags[:, 0:cap], cap), as_column(flags[:, middle : middle + cap], cap)], axis=0
    )
    heated = conv[:, :levels] + day * rad
    return jnp.concatenate([heated, conv[:, levels : 2 * levels]], axis=1).astype(jnp.bfloat16), updated


def rows_of(unit, cap):
    return pl.ds(pl.multiple_of(unit * 2 * cap, 2 * cap), 2 * cap)


def lower_kernel(cap, base, pick, low, targets_ref, packet_ref, cloud_ref, *refs):
    weights, refs = refs[:6], refs[6 + base :]
    (answer_ref, new_ref, first_ref), (updated_ref, sem) = refs[:3], refs[-2:]
    core, unit, _, inner = position()
    half, features = lax.axis_size("elem") // 4, packet_ref.shape[1]
    place = lax.bitwise_xor(inner, low)
    served = rows_of(place, cap)
    cloud = cloud_ref[served, :]
    answer_ref[...], updated_ref[...] = serve(cap, packet_ref, cloud, cloud_part(cloud, weights, features), weights)
    copy = pltpu.make_async_copy(updated_ref, new_ref.at[served, :], sem)
    copy.start()
    for j, part in enumerate(cloud_part(cloud_ref[rows_of(half + place, cap), :], weights, features)):
        first_ref[j] = part
    if pick:
        hot_ref = refs[3]
        table = jnp.transpose(targets_ref[...].astype(jnp.float32)).astype(jnp.int32)
        dest, order = table[:, 1:2], table[:, 2:3]
        step = lax.bitwise_xor(lax.shift_right_logical(dest, 1), jnp.full_like(dest, unit))
        side = jnp.where(lax.bitwise_and(dest, 1) == core, 0, 1)
        row = (step * 2 + side) * cap + order
        hot_ref[...] = (lax.broadcasted_iota(jnp.int32, hot_ref.shape, 1) == row).astype(jnp.bfloat16)
    copy.wait()


def upper_kernel(cap, low, lent_ref, lower_answer_ref, first_ref, cloud_ref, *refs):
    weights, (straight_ref, crossed_ref, new_ref) = refs[:6], refs[6:]
    _, _, upper, inner = position()
    upper_unit = lax.axis_size("elem") // 4 + lax.bitwise_xor(inner, low)
    answer, new_ref[...] = serve(cap, lent_ref, cloud_ref[rows_of(upper_unit, cap), :], first_ref, weights)

    @pl.when(upper == 0)
    def _():
        crossed_ref[...] = answer
        straight_ref[...] = lower_answer_ref[...]

    @pl.when(upper == 1)
    def _():
        straight_ref[...] = answer
        crossed_ref[...] = lower_answer_ref[...]


def store_kernel(cap, *refs):
    news, (new_ref, sems) = refs[:-3], refs[-2:]
    _, _, _, inner = position()
    copies = []
    for low, piece in enumerate(news):
        served = lax.axis_size("elem") // 4 + lax.bitwise_xor(inner, low)
        copies.append(pltpu.make_async_copy(piece, new_ref.at[rows_of(served, cap), :], sems.at[low]))
        copies[-1].start()
    for copy in copies:
        copy.wait()


def gathered(cap, hot_ref, pieces):
    total = None
    for place, blocks in pieces:
        block = blocks[0] if len(blocks) == 1 else jnp.concatenate(blocks, axis=0)
        part = dot(hot_ref[:, place * cap : (place + len(blocks)) * cap], block)
        total = part if total is None else total + part
    return total


def gather_kernel(cap, sequence, *refs):
    count = len(sequence)
    own, far, (hot_ref, out_ref) = refs[:count], refs[count:-2], refs[-2:]
    rows = pl.ds(pl.multiple_of(position()[0] * cap, cap), cap)
    pieces = []
    for i, du in enumerate(sequence):
        blocks = [own[i][rows, :]] + ([far[i][rows, :]] if i < count - 1 else [])
        pieces.append((2 * du, blocks))
    out_ref[...] = gathered(cap, hot_ref, pieces).astype(jnp.bfloat16)


def finish_kernel(cap, last, gathered_ref, far_ref, hot_ref, out_ref, buffer_ref, sems):
    block = far_ref[pl.ds(pl.multiple_of(position()[0] * cap, cap), cap), :]
    parts = sems.shape[0]
    step = out_ref.shape[0] // parts
    copies = []
    for i in range(parts):
        span = pl.ds(i * step, step)
        part = dot(hot_ref[span, (2 * last + 1) * cap : (2 * last + 2) * cap], block)
        buffer_ref[span, :] = (gathered_ref[span, :].astype(jnp.float32) + part).astype(jnp.bfloat16)
        copies.append(pltpu.make_async_copy(buffer_ref.at[span, :], out_ref.at[span, :], sems.at[i]))
        copies[-1].start()
    for copy in copies:
        copy.wait()


def per_device(state, dest_map, day_mask, cloud, conv_in, conv_mid, conv_out, rad_in, rad_mid, rad_out):
    groups, bands = lax.axis_size("elem"), lax.axis_size("band")
    units, half, away = groups // 2, groups // 4, bands // 2
    cap = cloud.shape[0] // groups
    columns, features = state.shape
    elem = lax.axis_index("elem")
    upper = elem // (groups // 2)
    vmem = pl.BlockSpec(memory_space=pltpu.VMEM)
    hbm = pl.BlockSpec(memory_space=pltpu.HBM)
    params = pltpu.CompilerParams(vmem_limit_bytes=VMEM_BYTES)
    weights = (conv_in, conv_mid, conv_out, rad_in, rad_mid, rad_out)

    def like(a):
        return jax.ShapeDtypeStruct(a.shape, a.dtype)

    def swapped(block):
        return moved(block, lambda e, b: (e ^ 1, b))

    dest_table, day_table = dest_map.reshape(columns // 128, 128), day_mask.reshape(columns // 128, 128)
    far_state = swapped(state)
    far_dest, far_day = swapped(dest_table), swapped(day_table)

    packet = jax.ShapeDtypeStruct((2 * cap + FLAG_ROWS, features), jnp.bfloat16)
    targets = pl.pallas_call(
        functools.partial(targets_kernel, groups, cap),
        out_shape=jax.ShapeDtypeStruct((8, columns), jnp.int32),
        in_specs=[vmem] * 2,
        out_specs=vmem,
        compiler_params=params,
        cost_estimate=work(4),
        name="column_targets",
    )(dest_table, far_dest)
    packets = [None] * units
    for chosen in ([half], [*range(half + 1, units), *range(half)]):
        earlier = [packets[half]] if packets[half] is not None else []
        outs = pl.pallas_call(
            functools.partial(place_kernel, cap, units, chosen[0]),
            out_shape=[packet] * len(chosen),
            in_specs=[vmem] * (5 + len(earlier)),
            out_specs=[vmem] * len(chosen),
            compiler_params=params,
            cost_estimate=work(3),
            name="place_columns",
        )(far_state, state, targets, far_day, day_table, *earlier)
        for du, out in zip(chosen, outs):
            packets[du] = out

    def onward(low, far):
        return lambda e, b: (e ^ (2 * low), (b + away * far) % bands)

    hopped = [moved(packets[half + low], onward(half, 0)) for low in range(half)]
    lent = [moved(jnp.where(upper == 0, hopped[low], packets[low]), onward(low, 1)) for low in range(half)]
    kept = [jnp.where(upper == 0, packets[low], hopped[low]) for low in range(half)]
    lower = [kept[low] if low == 0 else moved(kept[low], onward(low, 0)) for low in range(half)]

    tile = jax.ShapeDtypeStruct((2 * cap, features), jnp.bfloat16)
    new_tile = jax.ShapeDtypeStruct((2 * cap, cloud.shape[1]), jnp.bfloat16)
    first_shape = jax.ShapeDtypeStruct((2, 2 * cap, conv_in.shape[1]), jnp.float32)
    firsts = []
    hot_shape = jax.ShapeDtypeStruct((columns, groups * cap), jnp.bfloat16)
    answers, lower_answers, news, new_cloud = [None] * units, [], [], None
    for low in range(half):
        pick, base = low == 0, () if low == 0 else (new_cloud,)
        answer, new_cloud, first, *picked = pl.pallas_call(
            functools.partial(lower_kernel, cap, len(base), pick, low),
            out_shape=[tile, like(cloud), first_shape] + [hot_shape] * pick,
            in_specs=[vmem] * 9 + [hbm] * len(base),
            out_specs=[vmem, hbm, vmem] + [vmem] * pick,
            scratch_shapes=[pltpu.VMEM(new_tile.shape, jnp.bfloat16), pltpu.SemaphoreType.DMA],
            input_output_aliases={9: 1} if base else {},
            compiler_params=params,
            cost_estimate=work(3),
            name="lower_physics",
        )(targets, lower[low], cloud, *weights, *base)
        lower_answers.append(answer)
        firsts.append(first)
        if pick:
            hot = picked[0]
    for low in range(half):
        answers[low], answers[half + low], new = pl.pallas_call(
            functools.partial(upper_kernel, cap, low),
            out_shape=[tile, tile, new_tile],
            in_specs=[vmem] * 10,
            out_specs=[vmem] * 3,
            compiler_params=params,
            cost_estimate=work(3),
            name="upper_physics",
        )(lent[low], lower_answers[low], firsts[low], cloud, *weights)
        news.append(new)

    def home(du):
        def target(e, b):
            to_elem = e ^ (2 * du)
            return to_elem, (b + away) % bands if to_elem >= groups // 2 else b

        return target

    back = [None] * units
    sequence = [du for low in range(half) for du in (half + low, low)]
    back = [moved(answers[du], home(du)) for du in sequence]
    new_cloud = pl.pallas_call(
        functools.partial(store_kernel, cap),
        out_shape=like(cloud),
        in_specs=[vmem] * half + [hbm],
        out_specs=hbm,
        scratch_shapes=[pltpu.SemaphoreType.DMA((half,))],
        input_output_aliases={half: 0},
        compiler_params=params,
        cost_estimate=work(1),
        name="store_cloud",
    )(*news, new_cloud)
    back[0], new_cloud = lax.optimization_barrier((back[0], new_cloud))
    far_back = [swapped(block) for block in back]
    most = pl.pallas_call(
        functools.partial(gather_kernel, cap, sequence),
        out_shape=like(state),
        in_specs=[vmem] * (2 * units),
        out_specs=vmem,
        compiler_params=params,
        cost_estimate=work(2),
        name="gather_most",
    )(*back, *far_back[:-1], hot)
    tendency = pl.pallas_call(
        functools.partial(finish_kernel, cap, sequence[-1]),
        out_shape=like(state),
        in_specs=[vmem] * 3,
        out_specs=hbm,
        scratch_shapes=[pltpu.VMEM(state.shape, jnp.bfloat16), pltpu.SemaphoreType.DMA((2,))],
        compiler_params=params,
        cost_estimate=work(1),
        name="gather_last",
    )(most, far_back[-1], hot)
    return (tendency, new_cloud)


def solution(mesh):
    rows = P(("elem", "band"), None)
    return jax.shard_map(
        per_device,
        mesh=mesh,
        in_specs=(rows,) * 4 + (P(),) * 6,
        out_specs=(rows, rows),
        check_vma=False,
    )
```

```python
import functools

import jax
import jax.numpy as jnp
from jax import lax
from jax.experimental import pallas as pl
from jax.experimental.pallas import tpu as pltpu
from jax.sharding import PartitionSpec as P

VMEM_BYTES = 24 * 1024 * 1024
FLAG_ROWS = 16


def moved(block, target):
    groups, bands = lax.axis_size("elem"), lax.axis_size("band")
    route = []
    for e in range(groups):
        for b in range(bands):
            to = target(e, b)
            if to is not None:
                route.append((e * bands + b, to[0] * bands + to[1]))
    return lax.ppermute(block, ("elem", "band"), route)


def work(microseconds):
    return pl.CostEstimate(flops=int(microseconds * 1.15e9), bytes_accessed=0, transcendentals=0)


def position():
    elem, half = lax.axis_index("elem"), lax.axis_size("elem") // 4
    unit = elem // 2
    return elem % 2, unit, unit // half, unit % half


def dot(a, b):
    return jnp.dot(a, b, preferred_element_type=jnp.float32)


def as_row(table):
    return jnp.concatenate([table[r : r + 1, :] for r in range(table.shape[0])], axis=1)


def orders(dest, groups):
    count = dest.shape[1]
    lanes = 128
    hot = (lax.broadcasted_iota(jnp.int32, (groups, count), 0) == dest).astype(jnp.float32)
    before = (
        lax.broadcasted_iota(jnp.int32, (lanes, lanes), 0)
        < lax.broadcasted_iota(jnp.int32, (lanes, lanes), 1)
    ).astype(jnp.bfloat16)
    parts, seen = [], jnp.zeros((groups, 1), jnp.float32)
    for start in range(0, count, lanes):
        piece = hot[:, start : start + lanes]
        inside = dot(piece.astype(jnp.bfloat16), before)
        parts.append(jnp.sum(piece * (inside + seen), axis=0, keepdims=True))
        seen = seen + jnp.sum(piece, axis=1, keepdims=True)
    return jnp.concatenate(parts, axis=1).astype(jnp.int32)


def targets_kernel(groups, cap, dest_ref, far_dest_ref, out_ref):
    core, unit, _, _ = position()
    rows = []
    for dest_table in (dest_ref, far_dest_ref):
        dest = as_row(dest_table[...])
        order = orders(dest, groups)
        step = lax.bitwise_xor(lax.shift_right_logical(dest, 1), jnp.full_like(dest, unit))
        rows += [jnp.where(lax.bitwise_and(dest, 1) == core, step * cap + order, -1), dest, order, dest]
    out_ref[...] = jnp.concatenate(rows, axis=0)


def place_kernel(cap, units, chosen, far_state_ref, state_ref, targets_ref, far_day_ref, day_ref, *refs):
    core, _, _, _ = position()
    half = units // 2
    split = [du % half == 0 for du in chosen]
    out_refs = refs[-(len(chosen) + sum(split)) :]
    columns, features = state_ref.shape
    middle = features // 2
    placed, flags = [], []
    for rows, dest_row, day_table in ((state_ref, 0, day_ref), (far_state_ref, 4, far_day_ref)):
        row, day = targets_ref[dest_row : dest_row + 1, :], as_row(day_table[...])
        row = jnp.where(row < chosen[0] * cap, jnp.where(row < 0, row, row + units * cap), row) - chosen[0] * cap
        hot = (lax.broadcasted_iota(jnp.int32, (len(chosen) * cap, columns), 0) == row).astype(jnp.bfloat16)
        sun = jnp.broadcast_to(day.astype(jnp.float32), (FLAG_ROWS, columns)).astype(jnp.bfloat16)
        marks = lax.dot_general(sun, hot, (((1,), (1,)), ((), ())), preferred_element_type=jnp.float32)
        flags.append(marks.astype(jnp.bfloat16))
        placed.append(dot(hot, rows[...]).astype(jnp.bfloat16))
    for first in range(2):

        @pl.when(core == first)
        def _():
            rest = list(out_refs)
            for i, parts in enumerate(split):
                span = slice(i * cap, (i + 1) * cap)
                last = rest[1] if parts else rest[0]
                below = last.shape[0] - FLAG_ROWS
                if cap < middle:
                    last[below:, :] = jnp.zeros((FLAG_ROWS, features), jnp.bfloat16)
                for source in range(2):
                    out_ref = rest[source] if parts else last
                    place = 0 if parts else source * cap
                    out_ref[place : place + cap, :] = placed[source ^ first][span, :]
                    last[below:, source * middle : source * middle + cap] = flags[source ^ first][:, span]
                rest = rest[2:] if parts else rest[1:]


def join(cap, packet_ref, parts):
    packet_ref[0:cap, :] = parts[0][...]
    packet_ref[cap:, :] = parts[1][...]


def silu(v):
    return (0.5 * v) * (1.0 + jnp.tanh(0.5 * v))


def as_column(row, cap):
    same = lax.broadcasted_iota(jnp.int32, (cap, cap), 0) == lax.broadcasted_iota(jnp.int32, (cap, cap), 1)
    return jnp.sum(jnp.where(same, jnp.broadcast_to(row, (cap, cap)), 0.0), axis=1, keepdims=True)


def cloud_part(cloud, weights, features):
    return [dot(cloud, weights[i][features:, :]) for i in (0, 3)]


def serve(cap, packet, cloud, first, weights):
    conv_in, conv_mid, conv_out, rad_in, rad_mid, rad_out = weights
    features, levels = packet.shape[1], rad_out.shape[1]
    state = packet[0 : 2 * cap, :]
    conv = silu(dot(state, conv_in[:features, :]) + first[0]).astype(jnp.bfloat16)
    rad = silu(dot(state, rad_in[:features, :]) + first[1]).astype(jnp.bfloat16)
    conv = silu(dot(conv, conv_mid[...])).astype(jnp.bfloat16)
    rad = silu(dot(rad, rad_mid[...])).astype(jnp.bfloat16)
    conv = dot(conv, conv_out[...])
    rad = dot(rad, rad_out[...])
    updated = (cloud.astype(jnp.float32) + conv[:, 2 * levels :]).astype(jnp.bfloat16)
    flags = packet[2 * cap : 2 * cap + FLAG_ROWS, :].astype(jnp.float32)[0:1, :]
    middle = features // 2
    day = jnp.concatenate(
        [as_column(flags[:, 0:cap], cap), as_column(flags[:, middle : middle + cap], cap)], axis=0
    )
    heated = conv[:, :levels] + day * rad
    return jnp.concatenate([heated, conv[:, levels : 2 * levels]], axis=1).astype(jnp.bfloat16), updated


def rows_of(unit, cap):
    return pl.ds(pl.multiple_of(unit * 2 * cap, 2 * cap), 2 * cap)


def lower_kernel(cap, targets_ref, first_part, second_part, cloud_ref, *refs):
    weights, (answer_ref, new_ref, hot_ref), refs = refs[:6], refs[6:9], refs[9:]
    refs, (packet_ref, updated_ref, sem) = refs[:-3], refs[-3:]
    low_firsts, up_firsts = refs[: len(refs) // 2], refs[len(refs) // 2 :]
    join(cap, packet_ref, (first_part, second_part))
    core, unit, _, inner = position()
    half, features = lax.axis_size("elem") // 4, packet_ref.shape[1]
    served = rows_of(inner, cap)
    cloud = cloud_ref[served, :]
    answer_ref[...], updated_ref[...] = serve(cap, packet_ref, cloud, cloud_part(cloud, weights, features), weights)
    copy = pltpu.make_async_copy(updated_ref, new_ref.at[served, :], sem)
    copy.start()
    for base, lows, firsts in ((0, range(1, half), low_firsts), (half, range(half), up_firsts)):
        for low, first_ref in zip(lows, firsts):
            cloud = cloud_ref[rows_of(base + lax.bitwise_xor(inner, low), cap), :]
            for j, part in enumerate(cloud_part(cloud, weights, features)):
                first_ref[j] = part
    table = jnp.transpose(targets_ref[...].astype(jnp.float32)).astype(jnp.int32)
    dest, order = table[:, 1:2], table[:, 2:3]
    step = lax.bitwise_xor(lax.shift_right_logical(dest, 1), jnp.full_like(dest, unit))
    side = jnp.where(lax.bitwise_and(dest, 1) == core, 0, 1)
    row = (step * 2 + side) * cap + order
    hot_ref[...] = (lax.broadcasted_iota(jnp.int32, hot_ref.shape, 1) == row).astype(jnp.bfloat16)
    copy.wait()


def upper_kernel(cap, first_part, second_part, lower_answer_ref, first_ref, cloud_ref, *refs):
    weights, (straight_ref, crossed_ref, new_ref, packet_ref) = refs[:6], refs[6:]
    _, _, upper, inner = position()
    join(cap, packet_ref, (first_part, second_part))
    served = rows_of(lax.axis_size("elem") // 4 + inner, cap)
    answer, new_ref[...] = serve(cap, packet_ref, cloud_ref[served, :], first_ref, weights)

    @pl.when(upper == 0)
    def _():
        crossed_ref[...] = answer
        straight_ref[...] = lower_answer_ref[...]

    @pl.when(upper == 1)
    def _():
        straight_ref[...] = answer
        crossed_ref[...] = lower_answer_ref[...]


def both_kernel(cap, low, lower_ref, lent_ref, first_ref, lower_first_ref, cloud_ref, *refs):
    weights, (straight_ref, crossed_ref, new_ref, lower_new_ref) = refs[:6], refs[6:]
    _, _, upper, inner = position()
    place, half = lax.bitwise_xor(inner, low), lax.axis_size("elem") // 4
    answer, new_ref[...] = serve(cap, lent_ref, cloud_ref[rows_of(half + place, cap), :], first_ref, weights)
    lower, lower_new_ref[...] = serve(cap, lower_ref, cloud_ref[rows_of(place, cap), :], lower_first_ref, weights)

    @pl.when(upper == 0)
    def _():
        crossed_ref[...] = answer
        straight_ref[...] = lower

    @pl.when(upper == 1)
    def _():
        straight_ref[...] = answer
        crossed_ref[...] = lower


def store_kernel(cap, places, *refs):
    news, (new_ref, sems) = refs[:-3], refs[-2:]
    _, _, _, inner = position()
    copies = []
    for i, (piece, (base, low)) in enumerate(zip(news, places)):
        served = base + lax.bitwise_xor(inner, low)
        copies.append(pltpu.make_async_copy(piece, new_ref.at[rows_of(served, cap), :], sems.at[i]))
        copies[-1].start()
    for copy in copies:
        copy.wait()


def gathered(cap, hot_ref, pieces):
    total = None
    for place, blocks in pieces:
        block = blocks[0] if len(blocks) == 1 else jnp.concatenate(blocks, axis=0)
        part = dot(hot_ref[:, place * cap : (place + len(blocks)) * cap], block)
        total = part if total is None else total + part
    return total


def gather_kernel(cap, sequence, *refs):
    count = len(sequence)
    own, far, (hot_ref, out_ref) = refs[:count], refs[count:-2], refs[-2:]
    rows = pl.ds(pl.multiple_of(position()[0] * cap, cap), cap)
    pieces = []
    for i, du in enumerate(sequence):
        blocks = [own[i][rows, :]] + ([far[i][rows, :]] if i < count - 1 else [])
        pieces.append((2 * du, blocks))
    out_ref[...] = gathered(cap, hot_ref, pieces).astype(jnp.bfloat16)


def finish_kernel(cap, last, gathered_ref, far_ref, hot_ref, out_ref, buffer_ref, sems):
    block = far_ref[pl.ds(pl.multiple_of(position()[0] * cap, cap), cap), :]
    parts = sems.shape[0]
    step = out_ref.shape[0] // parts
    copies = []
    for i in range(parts):
        span = pl.ds(i * step, step)
        part = dot(hot_ref[span, (2 * last + 1) * cap : (2 * last + 2) * cap], block)
        buffer_ref[span, :] = (gathered_ref[span, :].astype(jnp.float32) + part).astype(jnp.bfloat16)
        copies.append(pltpu.make_async_copy(buffer_ref.at[span, :], out_ref.at[span, :], sems.at[i]))
        copies[-1].start()
    for copy in copies:
        copy.wait()


def per_device(state, dest_map, day_mask, cloud, conv_in, conv_mid, conv_out, rad_in, rad_mid, rad_out):
    groups, bands = lax.axis_size("elem"), lax.axis_size("band")
    units, half, away = groups // 2, groups // 4, bands // 2
    cap = cloud.shape[0] // groups
    columns, features = state.shape
    elem = lax.axis_index("elem")
    upper = elem // (groups // 2)
    vmem = pl.BlockSpec(memory_space=pltpu.VMEM)
    hbm = pl.BlockSpec(memory_space=pltpu.HBM)
    params = pltpu.CompilerParams(vmem_limit_bytes=VMEM_BYTES)
    weights = (conv_in, conv_mid, conv_out, rad_in, rad_mid, rad_out)

    def like(a):
        return jax.ShapeDtypeStruct(a.shape, a.dtype)

    def swapped(block):
        return moved(block, lambda e, b: (e ^ 1, b))

    dest_table, day_table = dest_map.reshape(columns // 128, 128), day_mask.reshape(columns // 128, 128)
    far_state = swapped(state)
    far_dest, far_day = swapped(dest_table), swapped(day_table)

    packet = jax.ShapeDtypeStruct((2 * cap + FLAG_ROWS, features), jnp.bfloat16)
    targets = pl.pallas_call(
        functools.partial(targets_kernel, groups, cap),
        out_shape=jax.ShapeDtypeStruct((8, columns), jnp.int32),
        in_specs=[vmem] * 2,
        out_specs=vmem,
        compiler_params=params,
        cost_estimate=work(4),
        name="column_targets",
    )(dest_table, far_dest)
    parts = [jax.ShapeDtypeStruct((cap + rows, features), jnp.bfloat16) for rows in (0, FLAG_ROWS)]
    packets = [None] * units
    for chosen in ([half], [*range(half + 1, units), *range(half)]):
        earlier = packets[half][:1] if packets[half] else []
        shapes = [parts if du % half == 0 else [packet] for du in chosen]
        outs = pl.pallas_call(
            functools.partial(place_kernel, cap, units, chosen),
            out_shape=sum(shapes, []),
            in_specs=[vmem] * (5 + len(earlier)),
            out_specs=[vmem] * sum(map(len, shapes)),
            compiler_params=params,
            cost_estimate=work(3),
            name="place_columns",
        )(far_state, state, targets, far_day, day_table, *earlier)
        for du, pieces in zip(chosen, shapes):
            packets[du], outs = outs[: len(pieces)], outs[len(pieces) :]

    def onward(low, far):
        return lambda e, b: (e ^ (2 * low), (b + away * far) % bands)

    def each(route, blocks):
        return [moved(block, route) for block in blocks]

    def chosen_of(side, yes, no):
        return [jnp.where(upper == side, a, b) for a, b in zip(yes, no)]

    hopped = [each(onward(half, 0), packets[half + low]) for low in range(half)]
    lent = [each(onward(low, 1), chosen_of(0, hopped[low], packets[low])) for low in range(half)]
    kept = [chosen_of(0, packets[low], hopped[low]) for low in range(half)]
    lower = [kept[low] if low == 0 else each(onward(low, 0), kept[low]) for low in range(half)]

    packet_buffer = pltpu.VMEM(packet.shape, jnp.bfloat16)
    tile = jax.ShapeDtypeStruct((2 * cap, features), jnp.bfloat16)
    new_tile = jax.ShapeDtypeStruct((2 * cap, cloud.shape[1]), jnp.bfloat16)
    first_shape = jax.ShapeDtypeStruct((2, 2 * cap, conv_in.shape[1]), jnp.float32)
    hot_shape = jax.ShapeDtypeStruct((columns, groups * cap), jnp.bfloat16)
    answers = [None] * units
    lower_answer, new_cloud, hot, *firsts = pl.pallas_call(
        functools.partial(lower_kernel, cap),
        out_shape=[tile, like(cloud), hot_shape] + [first_shape] * (units - 1),
        in_specs=[vmem] * 10,
        out_specs=[vmem, hbm] + [vmem] * units,
        scratch_shapes=[packet_buffer, pltpu.VMEM(new_tile.shape, jnp.bfloat16), pltpu.SemaphoreType.DMA],
        compiler_params=params,
        cost_estimate=work(3),
        name="lower_physics",
    )(targets, *lower[0], cloud, *weights)
    low_firsts, up_firsts = [None] + firsts[: half - 1], firsts[half - 1 :]
    answers[0], answers[half], new = pl.pallas_call(
        functools.partial(upper_kernel, cap),
        out_shape=[tile, tile, new_tile],
        in_specs=[vmem] * 11,
        out_specs=[vmem] * 3,
        scratch_shapes=[packet_buffer],
        compiler_params=params,
        cost_estimate=work(3),
        name="upper_physics",
    )(*lent[0], lower_answer, up_firsts[0], cloud, *weights)
    news, places = [new], [(half, 0)]
    for low in range(1, half):
        answers[low], answers[half + low], *both = pl.pallas_call(
            functools.partial(both_kernel, cap, low),
            out_shape=[tile, tile, new_tile, new_tile],
            in_specs=[vmem] * 11,
            out_specs=[vmem] * 4,
            compiler_params=params,
            cost_estimate=work(3),
            name="both_physics",
        )(*lower[low], *lent[low], up_firsts[low], low_firsts[low], cloud, *weights)
        news += both
        places += [(half, low), (0, low)]

    def home(du):
        def target(e, b):
            to_elem = e ^ (2 * du)
            return to_elem, (b + away) % bands if to_elem >= groups // 2 else b

        return target

    back = [None] * units
    sequence = [du for low in range(half) for du in (half + low, low)]
    back = [moved(answers[du], home(du)) for du in sequence]
    new_cloud = pl.pallas_call(
        functools.partial(store_kernel, cap, places),
        out_shape=like(cloud),
        in_specs=[vmem] * len(news) + [hbm],
        out_specs=hbm,
        scratch_shapes=[pltpu.SemaphoreType.DMA((len(news),))],
        input_output_aliases={len(news): 0},
        compiler_params=params,
        cost_estimate=work(0.01),
        name="store_cloud",
    )(*news, new_cloud)
    back[0], new_cloud = lax.optimization_barrier((back[0], new_cloud))
    far_back = [swapped(block) for block in back]
    most = pl.pallas_call(
        functools.partial(gather_kernel, cap, sequence),
        out_shape=like(state),
        in_specs=[vmem] * (2 * units),
        out_specs=vmem,
        compiler_params=params,
        cost_estimate=work(0.01),
        name="gather_most",
    )(*back, *far_back[:-1], hot)
    tendency = pl.pallas_call(
        functools.partial(finish_kernel, cap, sequence[-1]),
        out_shape=like(state),
        in_specs=[vmem] * 3,
        out_specs=hbm,
        scratch_shapes=[pltpu.VMEM(state.shape, jnp.bfloat16), pltpu.SemaphoreType.DMA((2,))],
        compiler_params=params,
        cost_estimate=work(0.01),
        name="gather_last",
    )(most, far_back[-1], hot)
    return (tendency, new_cloud)


def solution(mesh):
    rows = P(("elem", "band"), None)
    return jax.shard_map(
        per_device,
        mesh=mesh,
        in_specs=(rows,) * 4 + (P(),) * 6,
        out_specs=(rows, rows),
        check_vma=False,
    )
```

```python
import functools

import jax
import jax.numpy as jnp
from jax import lax
from jax.experimental import pallas as pl
from jax.experimental.pallas import tpu as pltpu
from jax.sharding import PartitionSpec as P

VMEM_BYTES = 24 * 1024 * 1024
FLAG_ROWS = 16


def moved(block, target):
    groups, bands = lax.axis_size("elem"), lax.axis_size("band")
    route = []
    for e in range(groups):
        for b in range(bands):
            to = target(e, b)
            if to is not None:
                route.append((e * bands + b, to[0] * bands + to[1]))
    return lax.ppermute(block, ("elem", "band"), route)


def work(microseconds):
    return pl.CostEstimate(flops=int(microseconds * 1.15e9), bytes_accessed=0, transcendentals=0)


def position():
    elem, half = lax.axis_index("elem"), lax.axis_size("elem") // 4
    unit = elem // 2
    return elem % 2, unit, unit // half, unit % half


def dot(a, b):
    return jnp.dot(a, b, preferred_element_type=jnp.float32)


def as_row(table):
    return jnp.concatenate([table[r : r + 1, :] for r in range(table.shape[0])], axis=1)


def orders(dest, groups):
    count = dest.shape[1]
    lanes = 128
    hot = (lax.broadcasted_iota(jnp.int32, (groups, count), 0) == dest).astype(jnp.float32)
    before = (
        lax.broadcasted_iota(jnp.int32, (lanes, lanes), 0)
        < lax.broadcasted_iota(jnp.int32, (lanes, lanes), 1)
    ).astype(jnp.bfloat16)
    parts, seen = [], jnp.zeros((groups, 1), jnp.float32)
    for start in range(0, count, lanes):
        piece = hot[:, start : start + lanes]
        inside = dot(piece.astype(jnp.bfloat16), before)
        parts.append(jnp.sum(piece * (inside + seen), axis=0, keepdims=True))
        seen = seen + jnp.sum(piece, axis=1, keepdims=True)
    return jnp.concatenate(parts, axis=1).astype(jnp.int32)


def targets_kernel(groups, cap, dest_ref, far_dest_ref, out_ref):
    core, unit, _, _ = position()
    rows = []
    for dest_table in (dest_ref, far_dest_ref):
        dest = as_row(dest_table[...])
        order = orders(dest, groups)
        step = lax.bitwise_xor(lax.shift_right_logical(dest, 1), jnp.full_like(dest, unit))
        rows += [jnp.where(lax.bitwise_and(dest, 1) == core, step * cap + order, -1), dest, order, dest]
    out_ref[...] = jnp.concatenate(rows, axis=0)


def place_kernel(cap, units, chosen, far_state_ref, state_ref, targets_ref, far_day_ref, day_ref, *refs):
    core, _, _, _ = position()
    half = units // 2
    split = [du % half == 0 for du in chosen]
    out_refs = refs[-(len(chosen) + sum(split)) :]
    columns, features = state_ref.shape
    middle = features // 2
    placed, flags = [], []
    for rows, dest_row, day_table in ((state_ref, 0, day_ref), (far_state_ref, 4, far_day_ref)):
        row, day = targets_ref[dest_row : dest_row + 1, :], as_row(day_table[...])
        row = jnp.where(row < chosen[0] * cap, jnp.where(row < 0, row, row + units * cap), row) - chosen[0] * cap
        hot = (lax.broadcasted_iota(jnp.int32, (len(chosen) * cap, columns), 0) == row).astype(jnp.bfloat16)
        sun = jnp.broadcast_to(day.astype(jnp.float32), (FLAG_ROWS, columns)).astype(jnp.bfloat16)
        marks = lax.dot_general(sun, hot, (((1,), (1,)), ((), ())), preferred_element_type=jnp.float32)
        flags.append(marks.astype(jnp.bfloat16))
        placed.append(dot(hot, rows[...]).astype(jnp.bfloat16))
    for first in range(2):

        @pl.when(core == first)
        def _():
            rest = list(out_refs)
            for i, parts in enumerate(split):
                span = slice(i * cap, (i + 1) * cap)
                last = rest[1] if parts else rest[0]
                below = last.shape[0] - FLAG_ROWS
                if cap < middle:
                    last[below:, :] = jnp.zeros((FLAG_ROWS, features), jnp.bfloat16)
                for source in range(2):
                    out_ref = rest[source] if parts else last
                    place = 0 if parts else source * cap
                    out_ref[place : place + cap, :] = placed[source ^ first][span, :]
                    last[below:, source * middle : source * middle + cap] = flags[source ^ first][:, span]
                rest = rest[2:] if parts else rest[1:]


def join(cap, packet_ref, parts):
    packet_ref[0:cap, :] = parts[0][...]
    packet_ref[cap:, :] = parts[1][...]


def silu(v):
    return (0.5 * v) * (1.0 + jnp.tanh(0.5 * v))


def as_column(row, cap):
    same = lax.broadcasted_iota(jnp.int32, (cap, cap), 0) == lax.broadcasted_iota(jnp.int32, (cap, cap), 1)
    return jnp.sum(jnp.where(same, jnp.broadcast_to(row, (cap, cap)), 0.0), axis=1, keepdims=True)


def cloud_part(cloud, weights, features):
    return [dot(cloud, weights[i][features:, :]) for i in (0, 3)]


def serve(cap, packet, cloud, first, weights):
    conv_in, conv_mid, conv_out, rad_in, rad_mid, rad_out = weights
    features, levels = packet.shape[1], rad_out.shape[1]
    state = packet[0 : 2 * cap, :]
    conv = silu(dot(state, conv_in[:features, :]) + first[0]).astype(jnp.bfloat16)
    rad = silu(dot(state, rad_in[:features, :]) + first[1]).astype(jnp.bfloat16)
    conv = silu(dot(conv, conv_mid[...])).astype(jnp.bfloat16)
    rad = silu(dot(rad, rad_mid[...])).astype(jnp.bfloat16)
    conv = dot(conv, conv_out[...])
    rad = dot(rad, rad_out[...])
    updated = (cloud.astype(jnp.float32) + conv[:, 2 * levels :]).astype(jnp.bfloat16)
    flags = packet[2 * cap : 2 * cap + FLAG_ROWS, :].astype(jnp.float32)[0:1, :]
    middle = features // 2
    day = jnp.concatenate(
        [as_column(flags[:, 0:cap], cap), as_column(flags[:, middle : middle + cap], cap)], axis=0
    )
    heated = conv[:, :levels] + day * rad
    return jnp.concatenate([heated, conv[:, levels : 2 * levels]], axis=1).astype(jnp.bfloat16), updated


def rows_of(unit, cap):
    return pl.ds(pl.multiple_of(unit * 2 * cap, 2 * cap), 2 * cap)


def lower_kernel(cap, targets_ref, first_part, second_part, cloud_ref, *refs):
    weights, (answer_ref, new_ref, hot_ref), refs = refs[:6], refs[6:9], refs[9:]
    refs, (packet_ref, updated_ref, sem) = refs[:-3], refs[-3:]
    low_firsts, up_firsts = refs[: len(refs) // 2], refs[len(refs) // 2 :]
    join(cap, packet_ref, (first_part, second_part))
    core, unit, _, inner = position()
    half, features = lax.axis_size("elem") // 4, packet_ref.shape[1]
    served = rows_of(inner, cap)
    cloud = cloud_ref[served, :]
    answer_ref[...], updated_ref[...] = serve(cap, packet_ref, cloud, cloud_part(cloud, weights, features), weights)
    copy = pltpu.make_async_copy(updated_ref, new_ref.at[served, :], sem)
    copy.start()
    for base, lows, firsts in ((0, range(1, half), low_firsts), (half, range(half), up_firsts)):
        for low, first_ref in zip(lows, firsts):
            cloud = cloud_ref[rows_of(base + lax.bitwise_xor(inner, low), cap), :]
            for j, part in enumerate(cloud_part(cloud, weights, features)):
                first_ref[j] = part
    table = jnp.transpose(targets_ref[...].astype(jnp.float32)).astype(jnp.int32)
    dest, order = table[:, 1:2], table[:, 2:3]
    step = lax.bitwise_xor(lax.shift_right_logical(dest, 1), jnp.full_like(dest, unit))
    side = jnp.where(lax.bitwise_and(dest, 1) == core, 0, 1)
    row = (step * 2 + side) * cap + order
    hot_ref[...] = (lax.broadcasted_iota(jnp.int32, hot_ref.shape, 1) == row).astype(jnp.bfloat16)
    copy.wait()


def upper_kernel(cap, first_part, second_part, lower_answer_ref, first_ref, cloud_ref, *refs):
    weights, (straight_ref, crossed_ref, new_ref, packet_ref) = refs[:6], refs[6:]
    _, _, upper, inner = position()
    join(cap, packet_ref, (first_part, second_part))
    served = rows_of(lax.axis_size("elem") // 4 + inner, cap)
    answer, new_ref[...] = serve(cap, packet_ref, cloud_ref[served, :], first_ref, weights)

    @pl.when(upper == 0)
    def _():
        crossed_ref[...] = answer
        straight_ref[...] = lower_answer_ref[...]

    @pl.when(upper == 1)
    def _():
        straight_ref[...] = answer
        crossed_ref[...] = lower_answer_ref[...]


def both_kernel(cap, low, lower_ref, lent_ref, first_ref, lower_first_ref, cloud_ref, *refs):
    weights, (straight_ref, crossed_ref, new_ref, lower_new_ref) = refs[:6], refs[6:]
    _, _, upper, inner = position()
    place, half = lax.bitwise_xor(inner, low), lax.axis_size("elem") // 4
    answer, new_ref[...] = serve(cap, lent_ref, cloud_ref[rows_of(half + place, cap), :], first_ref, weights)
    lower, lower_new_ref[...] = serve(cap, lower_ref, cloud_ref[rows_of(place, cap), :], lower_first_ref, weights)

    @pl.when(upper == 0)
    def _():
        crossed_ref[...] = answer
        straight_ref[...] = lower

    @pl.when(upper == 1)
    def _():
        straight_ref[...] = answer
        crossed_ref[...] = lower


def store_kernel(cap, places, *refs):
    news, (new_ref, sems) = refs[:-3], refs[-2:]
    _, _, _, inner = position()
    copies = []
    for i, (piece, (base, low)) in enumerate(zip(news, places)):
        served = base + lax.bitwise_xor(inner, low)
        copies.append(pltpu.make_async_copy(piece, new_ref.at[rows_of(served, cap), :], sems.at[i]))
        copies[-1].start()
    for copy in copies:
        copy.wait()


def gathered(cap, hot_ref, pieces):
    total = None
    for place, blocks in pieces:
        block = blocks[0] if len(blocks) == 1 else jnp.concatenate(blocks, axis=0)
        part = dot(hot_ref[:, place * cap : (place + len(blocks)) * cap], block)
        total = part if total is None else total + part
    return total


def gather_kernel(cap, sequence, *refs):
    count = len(sequence)
    own, far, (hot_ref, out_ref) = refs[:count], refs[count:-2], refs[-2:]
    rows = pl.ds(pl.multiple_of(position()[0] * cap, cap), cap)
    pieces = []
    for i, du in enumerate(sequence):
        blocks = [own[i][rows, :]] + ([far[i][rows, :]] if i < count - 1 else [])
        pieces.append((2 * du, blocks))
    out_ref[...] = gathered(cap, hot_ref, pieces).astype(jnp.bfloat16)


def finish_kernel(cap, last, gathered_ref, far_ref, hot_ref, out_ref, buffer_ref, sems):
    block = far_ref[...]
    parts = sems.shape[0]
    step = out_ref.shape[0] // parts
    copies = []
    for i in range(parts):
        span = pl.ds(i * step, step)
        part = dot(hot_ref[span, (2 * last + 1) * cap : (2 * last + 2) * cap], block)
        buffer_ref[span, :] = (gathered_ref[span, :].astype(jnp.float32) + part).astype(jnp.bfloat16)
        copies.append(pltpu.make_async_copy(buffer_ref.at[span, :], out_ref.at[span, :], sems.at[i]))
        copies[-1].start()
    for copy in copies:
        copy.wait()


def per_device(state, dest_map, day_mask, cloud, conv_in, conv_mid, conv_out, rad_in, rad_mid, rad_out):
    groups, bands = lax.axis_size("elem"), lax.axis_size("band")
    units, half, away = groups // 2, groups // 4, bands // 2
    cap = cloud.shape[0] // groups
    columns, features = state.shape
    elem = lax.axis_index("elem")
    upper = elem // (groups // 2)
    vmem = pl.BlockSpec(memory_space=pltpu.VMEM)
    hbm = pl.BlockSpec(memory_space=pltpu.HBM)
    params = pltpu.CompilerParams(vmem_limit_bytes=VMEM_BYTES)
    weights = (conv_in, conv_mid, conv_out, rad_in, rad_mid, rad_out)

    def like(a):
        return jax.ShapeDtypeStruct(a.shape, a.dtype)

    def swapped(block):
        return moved(block, lambda e, b: (e ^ 1, b))

    dest_table, day_table = dest_map.reshape(columns // 128, 128), day_mask.reshape(columns // 128, 128)
    far_state = swapped(state)
    far_dest, far_day = swapped(dest_table), swapped(day_table)

    packet = jax.ShapeDtypeStruct((2 * cap + FLAG_ROWS, features), jnp.bfloat16)
    targets = pl.pallas_call(
        functools.partial(targets_kernel, groups, cap),
        out_shape=jax.ShapeDtypeStruct((8, columns), jnp.int32),
        in_specs=[vmem] * 2,
        out_specs=vmem,
        compiler_params=params,
        cost_estimate=work(4),
        name="column_targets",
    )(dest_table, far_dest)
    parts = [jax.ShapeDtypeStruct((cap + rows, features), jnp.bfloat16) for rows in (0, FLAG_ROWS)]
    packets = [None] * units
    for chosen in ([half], [*range(half + 1, units), *range(half)]):
        earlier = packets[half][:1] if packets[half] else []
        shapes = [parts if du % half == 0 else [packet] for du in chosen]
        outs = pl.pallas_call(
            functools.partial(place_kernel, cap, units, chosen),
            out_shape=sum(shapes, []),
            in_specs=[vmem] * (5 + len(earlier)),
            out_specs=[vmem] * sum(map(len, shapes)),
            compiler_params=params,
            cost_estimate=work(3),
            name="place_columns",
        )(far_state, state, targets, far_day, day_table, *earlier)
        for du, pieces in zip(chosen, shapes):
            packets[du], outs = outs[: len(pieces)], outs[len(pieces) :]

    def onward(low, far):
        return lambda e, b: (e ^ (2 * low), (b + away * far) % bands)

    def each(route, blocks):
        return [moved(block, route) for block in blocks]

    def chosen_of(side, yes, no):
        return [jnp.where(upper == side, a, b) for a, b in zip(yes, no)]

    hopped = [each(onward(half, 0), packets[half + low]) for low in range(half)]
    lent = [each(onward(low, 1), chosen_of(0, hopped[low], packets[low])) for low in range(half)]
    kept = [chosen_of(0, packets[low], hopped[low]) for low in range(half)]
    lower = [kept[low] if low == 0 else each(onward(low, 0), kept[low]) for low in range(half)]

    packet_buffer = pltpu.VMEM(packet.shape, jnp.bfloat16)
    tile = jax.ShapeDtypeStruct((2 * cap, features), jnp.bfloat16)
    new_tile = jax.ShapeDtypeStruct((2 * cap, cloud.shape[1]), jnp.bfloat16)
    first_shape = jax.ShapeDtypeStruct((2, 2 * cap, conv_in.shape[1]), jnp.float32)
    hot_shape = jax.ShapeDtypeStruct((columns, groups * cap), jnp.bfloat16)
    answers = [None] * units
    lower_answer, new_cloud, hot, *firsts = pl.pallas_call(
        functools.partial(lower_kernel, cap),
        out_shape=[tile, like(cloud), hot_shape] + [first_shape] * (units - 1),
        in_specs=[vmem] * 10,
        out_specs=[vmem, hbm] + [vmem] * units,
        scratch_shapes=[packet_buffer, pltpu.VMEM(new_tile.shape, jnp.bfloat16), pltpu.SemaphoreType.DMA],
        compiler_params=params,
        cost_estimate=work(3),
        name="lower_physics",
    )(targets, *lower[0], cloud, *weights)
    low_firsts, up_firsts = [None] + firsts[: half - 1], firsts[half - 1 :]
    answers[0], answers[half], new = pl.pallas_call(
        functools.partial(upper_kernel, cap),
        out_shape=[tile, tile, new_tile],
        in_specs=[vmem] * 11,
        out_specs=[vmem] * 3,
        scratch_shapes=[packet_buffer],
        compiler_params=params,
        cost_estimate=work(3),
        name="upper_physics",
    )(*lent[0], lower_answer, up_firsts[0], cloud, *weights)
    news, places = [new], [(half, 0)]
    for low in range(1, half):
        answers[low], answers[half + low], *both = pl.pallas_call(
            functools.partial(both_kernel, cap, low),
            out_shape=[tile, tile, new_tile, new_tile],
            in_specs=[vmem] * 11,
            out_specs=[vmem] * 4,
            compiler_params=params,
            cost_estimate=work(3),
            name="both_physics",
        )(*lower[low], *lent[low], up_firsts[low], low_firsts[low], cloud, *weights)
        news += both
        places += [(half, low), (0, low)]

    def home(du):
        def target(e, b):
            to_elem = e ^ (2 * du)
            return to_elem, (b + away) % bands if to_elem >= groups // 2 else b

        return target

    back = [None] * units
    sequence = [du for low in range(half) for du in (half + low, low)]
    back = [moved(answers[du], home(du)) for du in sequence]
    new_cloud = pl.pallas_call(
        functools.partial(store_kernel, cap, places),
        out_shape=like(cloud),
        in_specs=[vmem] * len(news) + [hbm],
        out_specs=hbm,
        scratch_shapes=[pltpu.SemaphoreType.DMA((len(news),))],
        input_output_aliases={len(news): 0},
        compiler_params=params,
        cost_estimate=work(0.01),
        name="store_cloud",
    )(*news, new_cloud)
    back[0], new_cloud = lax.optimization_barrier((back[0], new_cloud))
    last_rows = lax.dynamic_slice_in_dim(back[-1], (1 - elem % 2) * cap, cap, axis=0)
    far_back = [swapped(block) for block in back[:-1] + [last_rows]]
    most = pl.pallas_call(
        functools.partial(gather_kernel, cap, sequence),
        out_shape=like(state),
        in_specs=[vmem] * (2 * units),
        out_specs=vmem,
        compiler_params=params,
        cost_estimate=work(0.01),
        name="gather_most",
    )(*back, *far_back[:-1], hot)
    tendency = pl.pallas_call(
        functools.partial(finish_kernel, cap, sequence[-1]),
        out_shape=like(state),
        in_specs=[vmem] * 3,
        out_specs=hbm,
        scratch_shapes=[pltpu.VMEM(state.shape, jnp.bfloat16), pltpu.SemaphoreType.DMA((2,))],
        compiler_params=params,
        cost_estimate=work(0.01),
        name="gather_last",
    )(most, far_back[-1], hot)
    return (tendency, new_cloud)


def solution(mesh):
    rows = P(("elem", "band"), None)
    return jax.shard_map(
        per_device,
        mesh=mesh,
        in_specs=(rows,) * 4 + (P(),) * 6,
        out_specs=(rows, rows),
        check_vma=False,
    )
```
